512 devices in a mesh: seq: 32 (over y, x, core), dp: 16 (over z).
Axes of the slice: x: 4, y: 4, z: 16, core: 2. Of those that a mesh axis runs over, the one named last changes fastest.
Arguments:
- student_query: bfloat16 [16, 4096, 768], P('dp', 'seq'), may hold values from -40 to 40
- key_cache: bfloat16 [16, 4096, 768], P('dp', 'seq'), may hold values from -40 to 40
- value_cache: bfloat16 [16, 4096, 768], P('dp', 'seq'), may hold values from -6 to 6
- grad_rows: bfloat16 [16, 4096, 1536], P('dp', 'seq'), may hold values from -1.5 to 1.5
- out_weight: bfloat16 [768, 1536], P('dp'), may hold values from -0.21875 to 0.21875
- return_counts: int32 [16, 32, 32], P('dp'), may hold values from 0 to 8, as said below
- block_sizes: int32 [16, 5], P('dp'), may hold values from 0 to 1560, as said below
Outputs:
- grad_query: bfloat16 [16, 4096, 768], P('dp', 'seq')
- grad_out_weight: float32 [768, 1536], P('seq', 'dp')
The draws below stay inside these ranges and needn't reach their ends.
Inputs may be any that keep to these rules, and one draw needn't show every extreme that they name: return_counts[c, s, o] is the number of rows that teacher shard s holds for frame owner o in clip c; every shard holds 128 rows in all and every owner receives 128 rows in all. `block_sizes`: the window's frame blocks in order, summing to 4096: a first block of fewer than 1560 positions (possibly empty), then whole frames of 1560 positions, then the rest of the window, then empty blocks.
All inputs are finite; a program needn't handle non-finite values.
Results may differ from the reference program's by a relative error of at most 0.018.
Values may be sent and summed in bfloat16 or wider, within the bound.
No kernel may reach another device: no remote copies, remote signals or barrier semaphores. Data moves between devices by JAX's collectives and lax.ppermute only.
A program may use at most 64 MiB of HBM per device.

```python
import jax
import jax.numpy as jnp
from jax import lax

D = 1536
HEAD_DIM = 128
HEADS = 6
HEAD_WIDTH = 768
FRAME = 1560
TOK_DEV = 128
TOKENS = 4096
CLIPS = 16
CAP = 8
NBLK = 5
N_SEQ = 32


def draw_student_query(key, part):
    key = jax.random.fold_in(key, 1)
    values = jnp.clip(jax.random.normal(key, (CLIPS, TOKENS, HEADS * HEAD_DIM), jnp.float32), -6.0, 6.0)
    return values.astype(jnp.bfloat16)


def draw_key_cache(key, part):
    key = jax.random.fold_in(key, 2)
    values = jnp.clip(jax.random.normal(key, (CLIPS, TOKENS, HEADS * HEAD_DIM), jnp.float32), -6.0, 6.0)
    return values.astype(jnp.bfloat16)


def draw_return_counts(key, part):
    key = jax.random.fold_in(key, 3)
    spans = N_SEQ - 1
    remaining = TOK_DEV - CAP
    ladder = jnp.arange(spans + 1, dtype=jnp.int32)
    cumulative = remaining * ladder * (ladder + 1) // (spans * (spans + 1))
    rungs = cumulative[1:] - cumulative[:-1]

    def one_clip(clip_key):
        order_key, owner_key = jax.random.split(clip_key)
        shuffled = rungs[jax.random.permutation(order_key, spans)]
        profile = jnp.concatenate([jnp.array([CAP], jnp.int32), shuffled.astype(jnp.int32)])
        owner_rank = jax.random.permutation(owner_key, N_SEQ).astype(jnp.int32)
        senders = jnp.arange(N_SEQ, dtype=jnp.int32)
        return profile[(owner_rank[None, :] - senders[:, None]) % N_SEQ]
    return jax.vmap(one_clip)(jax.random.split(key, CLIPS)).astype(jnp.int32)


def draw_block_sizes(key, part):
    key = jax.random.fold_in(key, 4)
    lead_top = min(FRAME - 1, TOKENS - FRAME)
    leads = jax.random.randint(key, (CLIPS,), 0, lead_top + 1).astype(jnp.int32)
    index = jnp.arange(NBLK, dtype=jnp.int32)
    left = TOKENS - leads[:, None] - (index[None, :] - 1) * FRAME
    later = jnp.clip(left, 0, FRAME)
    return jnp.where(index[None, :] == 0, leads[:, None], later).astype(jnp.int32)


def level_of(rng, shape, cuts, least, largest):
    gain = 1.0
    for axis_at, blocks in cuts:
        steps = jax.random.uniform(jax.random.fold_in(jax.random.fold_in(rng, 6), axis_at), (blocks,), jnp.float32, least / len(cuts), largest / len(cuts))
        gain = gain * jnp.repeat(jnp.exp(steps), shape[axis_at] // blocks).reshape((-1,) + (1,) * (len(shape) - 1 - axis_at))
    return gain


def gaussian(key, dims, width, reach, pieces=(), kind=jnp.bfloat16):
    values = jax.random.normal(key, dims, jnp.float32) * width
    if len(pieces) > 0:
        values = level_of(key, dims, pieces, -0.22, 0.18) * values
    return jnp.clip(values, min=-reach, max=reach).astype(kind)


def setup_inputs(seed: int = 0) -> dict:
    splits = jax.random.split(jax.random.key(seed), 8)
    return {
        "student_query": draw_student_query(jax.random.fold_in(splits[7], 71), 0),
        "key_cache": draw_key_cache(jax.random.fold_in(splits[7], 71), 0),
        "value_cache": gaussian(splits[2], (CLIPS, TOKENS, HEAD_WIDTH), 1.0, 6.0, ((0, 16), (1, 32))),
        "grad_rows": gaussian(splits[3], (CLIPS, TOKENS, D), 0.25, 1.5, ((0, 16), (1, 32))),
        "out_weight": gaussian(splits[4], (HEAD_WIDTH, D), HEAD_WIDTH ** -0.5, 0.21875, ((0, 16),)),
        "return_counts": draw_return_counts(jax.random.fold_in(splits[7], 71), 0),
        "block_sizes": draw_block_sizes(jax.random.fold_in(splits[7], 71), 0),
    }


def reorder_rows(teacher_rows, counts):
    peer_count = counts.shape[0]
    row_count = teacher_rows.shape[0] // peer_count
    shard_ends = jnp.cumsum(counts, axis=1).astype(jnp.int32)
    shard_starts = (shard_ends - counts).astype(jnp.int32)
    owner_ends = jnp.cumsum(counts, axis=0).astype(jnp.int32)
    owner_starts = (owner_ends - counts).astype(jnp.int32)
    within = jnp.arange(row_count, dtype=jnp.int32)
    owner_of = jnp.sum((shard_ends[:, None, :] <= within[None, :, None]).astype(jnp.int32), axis=2).astype(jnp.int32)
    start_here = jnp.take_along_axis(shard_starts, owner_of, axis=1)
    offset_here = jnp.take_along_axis(owner_starts, owner_of, axis=1)
    target = (owner_of * row_count + offset_here + within[None, :] - start_here).astype(jnp.int32)
    placed = jnp.zeros_like(teacher_rows)
    return placed.at[target.reshape(-1)].set(teacher_rows)


def visible_limits(block_lengths, position_end):
    block_ends = jnp.cumsum(block_lengths).astype(jnp.int32)
    positions = jnp.arange(position_end, dtype=jnp.int32)
    return jnp.min(jnp.where(block_ends[None, :] > positions[:, None], block_ends[None, :], position_end), axis=1)


def head_pass(query_head, key_head, value_head, grad_head, limits):
    score_scale = HEAD_DIM ** -0.5
    scores = jnp.dot(query_head, key_head.T, preferred_element_type=jnp.float32) * score_scale
    visible = jnp.arange(key_head.shape[0], dtype=jnp.int32)[None, :] < limits[:, None]
    scores = jnp.where(visible, scores, -1e30)
    top_score = jnp.max(scores, axis=1, keepdims=True)
    weights = jnp.where(visible, jnp.exp(scores - top_score), 0.0)
    probs = weights / jnp.sum(weights, axis=1, keepdims=True)
    attended = jnp.dot(probs.astype(jnp.bfloat16), value_head, preferred_element_type=jnp.float32)
    grad_probs = jnp.dot(grad_head, value_head.T, preferred_element_type=jnp.float32)
    centre = jnp.sum(probs * grad_probs, axis=1, keepdims=True)
    grad_scores = (probs * (grad_probs - centre)).astype(jnp.bfloat16)
    grad_query = jnp.dot(grad_scores, key_head, preferred_element_type=jnp.float32) * score_scale
    return attended, grad_query


def reference(student_query, key_cache, value_cache, grad_rows, out_weight, return_counts, block_sizes):
    head_width = HEADS * HEAD_DIM

    def split_heads(matrix):
        return matrix.reshape(TOKENS, HEADS, HEAD_DIM).transpose(1, 0, 2)

    def join_heads(stacked):
        return stacked.transpose(1, 0, 2).reshape(TOKENS, head_width)

    def clip_pass(operands):
        queries, cache_keys, cache_values, teacher_rows, counts, block_lengths = operands
        ordered = reorder_rows(teacher_rows, counts)
        head_grad = lax.dot_general(ordered, out_weight, (((1,), (1,)), ((), ())), preferred_element_type=jnp.float32).astype(jnp.bfloat16)
        limits = visible_limits(block_lengths, TOKENS)
        attended, grad_heads = lax.map(
            lambda head_parts: head_pass(head_parts[0], head_parts[1], head_parts[2], head_parts[3], limits),
            (split_heads(queries), split_heads(cache_keys), split_heads(cache_values), split_heads(head_grad)))
        attended = join_heads(attended).astype(jnp.bfloat16)
        grad_query = join_heads(grad_heads).astype(jnp.bfloat16)
        owner_attended = attended.reshape(N_SEQ, TOK_DEV, head_width)
        owner_rows = ordered.reshape(N_SEQ, TOK_DEV, D)

        def add_owner(summed, blocks_in):
            term = lax.dot_general(blocks_in[0], blocks_in[1], (((0,), (0,)), ((), ())), preferred_element_type=jnp.float32)
            rounded = lax.optimization_barrier(term.astype(jnp.bfloat16)).astype(jnp.float32)
            return summed + rounded, None

        clip_total, _ = lax.scan(add_owner, jnp.zeros((head_width, D), jnp.float32), (owner_attended, owner_rows))
        return grad_query, clip_total

    grad_query, clip_totals = lax.map(clip_pass, (student_query, key_cache, value_cache, grad_rows, return_counts, block_sizes))
    return grad_query, jnp.sum(clip_totals, axis=0) / CLIPS
```

```python
import functools

import jax
import jax.numpy as jnp
from jax import lax
from jax.experimental import pallas as pl
from jax.experimental.pallas import tpu as pltpu
from jax.sharding import PartitionSpec as P

HEAD_DIM = 128
SIDE = 4
CORES = 2
LOG2_E = 1.4426950408889634
HIDDEN = -1e30
LOWEST = -1e20
MIB = 1024 * 1024
NT = (((1,), (1,)), ((), ()))
NN = (((1,), (0,)), ((), ()))


def moves(dy, dx, dcore):
    pairs = []
    for y in range(SIDE):
        for x in range(SIDE):
            for core in range(CORES):
                there = ((y + dy) % SIDE * SIDE + (x + dx) % SIDE) * CORES + (core + dcore) % CORES
                pairs.append(((y * SIDE + x) * CORES + core, there))
    return pairs


def send(value, dy=0, dx=0, dcore=0):
    return lax.ppermute(value, "seq", moves(dy, dx, dcore))


def tiles_of(refs):
    tiles = []
    for first in (0, 5):
        for place in range(3):
            tiles.append((refs[first + place].at[0], refs[first + place].at[1]))
        tiles.append((refs[first + 3], refs[first + 4]))
    return tiles


def forward_kernel(head_count, scale, limit_ref, place_ref, query_ref, *refs):
    tiles = tiles_of(refs[:10])
    attended_ref, exact_ref, level_ref = refs[10:]
    limits = limit_ref[...]
    rows = query_ref.shape[0]
    for head in range(head_count):
        columns = pl.ds(head * HEAD_DIM, HEAD_DIM)
        query = query_ref[:, columns]
        peak = jnp.full((rows, 1), LOWEST, jnp.float32)
        norm = jnp.zeros((rows, 1), jnp.float32)
        total = jnp.zeros((rows, HEAD_DIM), jnp.float32)
        for index, (key_ref, value_ref) in enumerate(tiles):
            scores = lax.dot_general(query, key_ref[:, columns], NT, preferred_element_type=jnp.float32)
            visible = place_ref[index : index + 1, :] < limits
            scores = jnp.where(visible, scores * (scale * LOG2_E), HIDDEN)
            new_peak = jnp.maximum(peak, jnp.max(scores, axis=1, keepdims=True))
            rescale = jnp.exp2(peak - new_peak)
            weights = jnp.exp2(scores - new_peak)
            norm = norm * rescale + jnp.sum(weights, axis=1, keepdims=True)
            total = total * rescale + lax.dot_general(
                weights.astype(jnp.bfloat16), value_ref[:, columns], NN, preferred_element_type=jnp.float32
            )
            peak = new_peak
        total = total / norm
        attended_ref[:, columns] = total.astype(jnp.bfloat16)
        exact_ref[:, columns] = total
        level_ref[:, columns] = jnp.broadcast_to(peak + jnp.log2(norm), (rows, HEAD_DIM))


def backward_kernel(head_count, scale, limit_ref, place_ref, query_ref, grad_ref, exact_ref, level_ref, *refs):
    tiles = tiles_of(refs[:10])
    out_ref = refs[10]
    limits = limit_ref[...]
    rows = query_ref.shape[0]
    for head in range(head_count):
        columns = pl.ds(head * HEAD_DIM, HEAD_DIM)
        query = query_ref[:, columns]
        grad = grad_ref[:, columns]
        level = level_ref[:, pl.ds(head * HEAD_DIM, 1)]
        centre = jnp.sum(grad.astype(jnp.float32) * exact_ref[:, columns], axis=1, keepdims=True)
        total = jnp.zeros((rows, HEAD_DIM), jnp.float32)
        for index, (key_ref, value_ref) in enumerate(tiles):
            keys = key_ref[:, columns]
            scores = lax.dot_general(query, keys, NT, preferred_element_type=jnp.float32)
            visible = place_ref[index : index + 1, :] < limits
            probs = jnp.exp2(jnp.where(visible, scores * (scale * LOG2_E) - level, HIDDEN))
            grad_probs = lax.dot_general(grad, value_ref[:, columns], NT, preferred_element_type=jnp.float32)
            grad_scores = (probs * (grad_probs - centre)).astype(jnp.bfloat16)
            total = total + lax.dot_general(grad_scores, keys, NN, preferred_element_type=jnp.float32)
        out_ref[:, columns] = (total * scale).astype(jnp.bfloat16)


def whole(count):
    return [pl.BlockSpec(memory_space=pltpu.VMEM)] * count


def order_rows(teacher_rows, counts, me):
    row_count, feature_count = teacher_rows.shape
    peer_count = counts.shape[0]
    capacity = 2 * row_count // peer_count
    mine = lax.dynamic_index_in_dim(counts, me, 0, keepdims=False)
    starts = jnp.cumsum(mine) - mine
    slot = jnp.arange(capacity, dtype=jnp.int32)
    source_row = jnp.minimum(starts[:, None] + slot[None, :], row_count - 1)
    packed = teacher_rows[source_row]
    arrived = lax.all_to_all(packed, "seq", split_axis=0, concat_axis=0, tiled=True)
    inbound = lax.dynamic_index_in_dim(counts, me, 1, keepdims=False)
    inbound_ends = jnp.cumsum(inbound)
    local_rows = jnp.arange(row_count, dtype=jnp.int32)
    earlier = inbound_ends[None, :] <= local_rows[:, None]
    sender = jnp.sum(earlier.astype(jnp.int32), axis=1)
    offset_in = local_rows - jnp.sum(jnp.where(earlier, inbound[None, :], 0), axis=1)
    return arrived.reshape(peer_count * capacity, feature_count)[sender * capacity + offset_in]


def shards(student_query, key_cache, value_cache, grad_rows, out_weight, return_counts, block_sizes):
    queries, keys, values = student_query[0], key_cache[0], value_cache[0]
    me = lax.axis_index("seq")
    core = me % CORES
    at_x = me // CORES % SIDE
    at_y = me // (CORES * SIDE)
    row_count, head_width = queries.shape
    width = head_width // CORES
    head_count = width // HEAD_DIM
    scale = HEAD_DIM ** -0.5
    peer_count = lax.axis_size("seq")
    clip_count = lax.axis_size("dp")

    def half(rows, which):
        return lax.dynamic_slice(rows, (0, which * width), (row_count, width))

    weight = lax.all_gather(out_weight, "dp", axis=0, tiled=True)
    mine = jnp.stack([half(keys, core), half(values, core)])
    swapped = send(jnp.stack([half(keys, 1 - core), half(values, 1 - core), half(queries, 1 - core)]), dcore=1)
    theirs = swapped[:2]
    query = jnp.concatenate([half(queries, core), swapped[2]], axis=0)

    def spread(block, first, second):
        row = jnp.concatenate(
            [block, send(block, **{first: 1}), send(block, **{first: -1}), send(block, **{first: 2})], axis=1
        )
        before = send(row, **{second: 1})
        after = send(row, **{second: -1})
        return [row, before, after, send(before[0], **{second: 1}), send(after[1], **{second: -1})]

    tiles = spread(mine, "dx", "dy") + spread(theirs, "dy", "dx")
    steps = jnp.array([0, -1, 1, 2], jnp.int32)
    near_y = (at_y + steps) % SIDE
    near_x = (at_x + steps) % SIDE
    seats = jnp.concatenate(
        [
            (near_y[:, None] * SIDE + near_x[None, :]) * CORES + core,
            (near_y[None, :] * SIDE + near_x[:, None]) * CORES + (1 - core),
        ],
        axis=0,
    )
    local_rows = jnp.arange(row_count, dtype=jnp.int32)
    places = (seats[:, :, None] * row_count + local_rows[None, None, :]).reshape(2 * SIDE, SIDE * row_count)

    block_ends = jnp.cumsum(block_sizes[0])
    positions = jnp.concatenate([me * row_count + local_rows, (me + 1 - 2 * core) * row_count + local_rows])
    limits = jnp.min(
        jnp.where(block_ends[None, :] > positions[:, None], block_ends[None, :], row_count * peer_count),
        axis=1,
        keepdims=True,
    )

    both = CORES * row_count
    attended, exact, level = pl.pallas_call(
        functools.partial(forward_kernel, head_count, scale),
        out_shape=[
            jax.ShapeDtypeStruct((both, width), jnp.bfloat16),
            jax.ShapeDtypeStruct((both, width), jnp.float32),
            jax.ShapeDtypeStruct((both, width), jnp.float32),
        ],
        in_specs=whole(13),
        out_specs=whole(3),
        compiler_params=pltpu.CompilerParams(vmem_limit_bytes=40 * MIB),
        cost_estimate=pl.CostEstimate(flops=int(8e9), bytes_accessed=int(8e6), transcendentals=0),
        name="attend",
    )(limits, places, query, *tiles)

    own_ordered = order_rows(grad_rows[0], return_counts[0], me)
    ordered = jnp.concatenate([own_ordered, send(own_ordered, dcore=1)], axis=0)
    partial_sum = lax.dot_general(
        attended, ordered, (((0,), (0,)), ((), ())), preferred_element_type=jnp.float32
    ).astype(jnp.bfloat16)
    chip_count = SIDE * SIDE
    share = width // chip_count
    groups = [[chip * CORES + which for chip in range(chip_count)] for which in range(CORES)]
    pieces = lax.all_to_all(
        partial_sum.reshape(chip_count, share, -1), "seq", 0, 0, axis_index_groups=groups, tiled=True
    )

    head_grad = lax.dot_general(
        ordered,
        lax.dynamic_slice_in_dim(weight, core * width, width, axis=0),
        NT,
        preferred_element_type=jnp.float32,
    ).astype(jnp.bfloat16)
    grad_query = pl.pallas_call(
        functools.partial(backward_kernel, head_count, scale),
        out_shape=jax.ShapeDtypeStruct((both, width), jnp.bfloat16),
        in_specs=whole(16),
        out_specs=pl.BlockSpec(memory_space=pltpu.VMEM),
        compiler_params=pltpu.CompilerParams(vmem_limit_bytes=40 * MIB),
        cost_estimate=pl.CostEstimate(flops=int(8e9), bytes_accessed=int(8e6), transcendentals=0),
        name="attend_grad",
    )(limits, places, query, head_grad, exact, level, *tiles)
    own_grad = grad_query[:row_count]
    other_grad = send(grad_query[row_count:], dcore=1)
    grad_query_rows = jnp.where(
        core == 0,
        jnp.concatenate([own_grad, other_grad], axis=1),
        jnp.concatenate([other_grad, own_grad], axis=1),
    )

    clip_sum = jnp.sum(pieces.astype(jnp.float32), axis=0)
    clip_parts = clip_sum.reshape(share, clip_count, -1).transpose(1, 0, 2)
    terms = lax.all_to_all(clip_parts, "dp", 0, 0, tiled=True)
    total = jnp.sum(terms, axis=0) / float(clip_count)
    total = lax.ppermute(
        total, "seq", [(chip * CORES + which, which * chip_count + chip) for chip in range(chip_count) for which in range(CORES)]
    )
    return (grad_query_rows[None], total)


def solution(mesh):
    in_specs = (
        P("dp", "seq", None),
        P("dp", "seq", None),
        P("dp", "seq", None),
        P("dp", "seq", None),
        P("dp", None),
        P("dp", None, None),
        P("dp", None),
    )
    out_specs = (P("dp", "seq", None), P("seq", "dp"))
    return jax.shard_map(shards, mesh=mesh, in_specs=in_specs, out_specs=out_specs, check_vma=False)
```

```python
import functools

import jax
import jax.numpy as jnp
from jax import lax
from jax.experimental import pallas as pl
from jax.experimental.pallas import tpu as pltpu
from jax.sharding import PartitionSpec as P

HEAD_DIM = 128
SIDE = 4
CORES = 2
PAIR = 2
SLOTS = SIDE * PAIR
QUERY_SLOTS = 2
KEY_SLOTS = 4
LOG2_E = 1.4426950408889634
HIDDEN = -1e30
LOWEST = -1e20
MIB = 1024 * 1024
NT = (((1,), (1,)), ((), ()))
NN = (((1,), (0,)), ((), ()))
TN = (((0,), (0,)), ((), ()))


def seat(y, x, core):
    return (y % SIDE * SIDE + x % SIDE) * CORES + core % CORES


def send(value, dx=0, dcore=0):
    pairs = [
        (seat(y, x, core), seat(y, x + dx, core + dcore))
        for y in range(SIDE)
        for x in range(SIDE)
        for core in range(CORES)
    ]
    return lax.ppermute(value, "seq", pairs)


def trade(slots):
    groups = [
        [seat(y, PAIR * side + x, core) for y in range(SIDE) for x in range(PAIR)]
        for side in range(SIDE // PAIR)
        for core in range(CORES)
    ]
    return lax.all_to_all(slots, "seq", 0, 0, axis_index_groups=groups, tiled=True)


def tiles_of(refs):
    return [
        (ref.at[pl.ds(first, KEY_SLOTS), 0], ref.at[pl.ds(first, KEY_SLOTS), 1])
        for ref in refs
        for first in range(0, SLOTS, KEY_SLOTS)
    ]


def rows_of(ref):
    return ref[...].reshape(-1, HEAD_DIM)


def attend_blocks(scale, first_tile, limit_ref, place_ref, input_ref, tiles, start, finish):
    for block in range(SLOTS // QUERY_SLOTS):
        slots = pl.ds(block * QUERY_SLOTS, QUERY_SLOTS)
        query = rows_of(input_ref.at[slots, 0])
        limits = limit_ref[slots].reshape(-1, 1)
        peak, norm, total = start(slots, query.shape[0])
        for index, (key_ref, value_ref) in enumerate(tiles):
            scores = lax.dot_general(query, rows_of(key_ref), NT, preferred_element_type=jnp.float32)
            visible = place_ref[first_tile + index : first_tile + index + 1, :] < limits
            scores = jnp.where(visible, scores * (scale * LOG2_E), HIDDEN)
            new_peak = jnp.maximum(peak, jnp.max(scores, axis=1, keepdims=True))
            rescale = jnp.exp2(peak - new_peak)
            weights = jnp.exp2(scores - new_peak)
            norm = norm * rescale + jnp.sum(weights, axis=1, keepdims=True)
            total = total * rescale + lax.dot_general(
                weights.astype(jnp.bfloat16), rows_of(value_ref), NN, preferred_element_type=jnp.float32
            )
            peak = new_peak
        finish(slots, peak, norm, total)


def split_rows(rows):
    return rows.reshape(QUERY_SLOTS, -1, rows.shape[1])


def near_kernel(scale, limit_ref, place_ref, input_ref, own_ref, core_ref, peak_ref, norm_ref, total_ref):
    def start(slots, rows):
        return (
            jnp.full((rows, 1), LOWEST, jnp.float32),
            jnp.zeros((rows, 1), jnp.float32),
            jnp.zeros((rows, HEAD_DIM), jnp.float32),
        )

    def finish(slots, peak, norm, total):
        peak_ref[slots] = split_rows(peak)
        norm_ref[slots] = split_rows(norm)
        total_ref[slots] = split_rows(total)

    attend_blocks(scale, 0, limit_ref, place_ref, input_ref, tiles_of([own_ref, core_ref]), start, finish)


def far_kernel(
    scale, limit_ref, place_ref, input_ref, own_ref, core_ref, peak_ref, norm_ref, total_ref, attended_ref, exact_ref, level_ref
):
    def start(slots, rows):
        return (
            peak_ref[slots].reshape(rows, 1),
            norm_ref[slots].reshape(rows, 1),
            total_ref[slots].reshape(rows, HEAD_DIM),
        )

    def finish(slots, peak, norm, total):
        total = total / norm
        attended_ref[slots] = split_rows(total.astype(jnp.bfloat16))
        exact_ref[slots] = split_rows(total)
        level_ref[slots] = split_rows(peak + jnp.log2(norm))

    tiles = tiles_of([own_ref, core_ref])
    attend_blocks(scale, len(tiles), limit_ref, place_ref, input_ref, tiles, start, finish)


def grad_kernel(
    scale, limit_ref, place_ref, input_ref, grad_ref, exact_ref, level_ref, own_ref, core_ref, far_ref, far_core_ref, out_ref
):
    tiles = tiles_of([own_ref, core_ref, far_ref, far_core_ref])
    for block in range(SLOTS // QUERY_SLOTS):
        slots = pl.ds(block * QUERY_SLOTS, QUERY_SLOTS)
        query = rows_of(input_ref.at[slots, 0])
        limits = limit_ref[slots].reshape(-1, 1)
        level = level_ref[slots].reshape(-1, 1)
        grad = rows_of(grad_ref.at[slots])
        centre = jnp.sum(grad.astype(jnp.float32) * rows_of(exact_ref.at[slots]), axis=1, keepdims=True)
        total = jnp.zeros((query.shape[0], HEAD_DIM), jnp.float32)
        for index, (key_ref, value_ref) in enumerate(tiles):
            keys = rows_of(key_ref)
            scores = lax.dot_general(query, keys, NT, preferred_element_type=jnp.float32)
            visible = place_ref[index : index + 1, :] < limits
            probs = jnp.exp2(jnp.where(visible, scores * (scale * LOG2_E) - level, HIDDEN))
            grad_probs = lax.dot_general(grad, rows_of(value_ref), NT, preferred_element_type=jnp.float32)
            grad_scores = (probs * (grad_probs - centre)).astype(jnp.bfloat16)
            total = total + lax.dot_general(grad_scores, keys, NN, preferred_element_type=jnp.float32)
        out_ref[slots] = split_rows((total * scale).astype(jnp.bfloat16))


def project_kernel(head_count, rows_ref, weight_ref, out_ref):
    rows = rows_ref[...]
    for slot in range(SLOTS):
        head = slot % head_count
        out_ref[slot] = lax.dot_general(
            rows, weight_ref[pl.ds(head * HEAD_DIM, HEAD_DIM), :], NT, preferred_element_type=jnp.float32
        ).astype(jnp.bfloat16)


def outer_kernel(own_ref, other_ref, own_rows_ref, other_rows_ref, out_ref):
    own_rows = own_rows_ref[...]
    other_rows = other_rows_ref[...]
    for head in range(own_ref.shape[0]):
        term = lax.dot_general(own_ref[head], own_rows, TN, preferred_element_type=jnp.float32)
        term = term + lax.dot_general(other_ref[head], other_rows, TN, preferred_element_type=jnp.float32)
        out_ref[pl.ds(head * HEAD_DIM, HEAD_DIM), :] = term.astype(jnp.bfloat16)


def pack_kernel(head_count, query_ref, key_ref, value_ref, out_ref):
    for slot in range(SLOTS):
        columns = pl.ds(slot % head_count * HEAD_DIM, HEAD_DIM)
        for place, ref in enumerate((query_ref, key_ref, value_ref)):
            out_ref[slot, place] = ref[0, :, columns]


def join_kernel(head_count, slots_ref, out_ref):
    for head in range(head_count):
        out_ref[0, :, pl.ds(head * HEAD_DIM, HEAD_DIM)] = slots_ref[head]


def sum_kernel(pieces_ref, out_ref):
    total = pieces_ref[0].astype(jnp.float32)
    for chip in range(1, pieces_ref.shape[0]):
        total = total + pieces_ref[chip].astype(jnp.float32)
    total = total.astype(jnp.bfloat16)
    width = out_ref.shape[2]
    for clip in range(out_ref.shape[0]):
        out_ref[clip] = total[:, clip * width : (clip + 1) * width]


def call(kernel, out_shape, name, flops):
    def run(*operands):
        return pl.pallas_call(
            kernel,
            out_shape=[jax.ShapeDtypeStruct(shape, dtype) for shape, dtype in out_shape],
            in_specs=[pl.BlockSpec(memory_space=pltpu.VMEM)] * len(operands),
            out_specs=[pl.BlockSpec(memory_space=pltpu.VMEM)] * len(out_shape),
            compiler_params=pltpu.CompilerParams(vmem_limit_bytes=24 * MIB),
            cost_estimate=pl.CostEstimate(flops=int(flops), bytes_accessed=int(1e6), transcendentals=0),
            name=name,
        )(*operands)

    return run


def pack_rows(teacher_rows, counts, me):
    row_count = teacher_rows.shape[0]
    capacity = 2 * row_count // counts.shape[0]
    mine = lax.dynamic_index_in_dim(counts, me, 0, keepdims=False)
    starts = jnp.cumsum(mine) - mine
    slot = jnp.arange(capacity, dtype=jnp.int32)
    source_row = jnp.minimum(starts[:, None] + slot[None, :], row_count - 1)
    return teacher_rows[source_row]


def unpack_rows(arrived, counts, me, row_count):
    peer_count, capacity, feature_count = arrived.shape
    inbound = lax.dynamic_index_in_dim(counts, me, 1, keepdims=False)
    inbound_ends = jnp.cumsum(inbound)
    local_rows = jnp.arange(row_count, dtype=jnp.int32)
    earlier = inbound_ends[None, :] <= local_rows[:, None]
    sender = jnp.sum(earlier.astype(jnp.int32), axis=1)
    offset_in = local_rows - jnp.sum(jnp.where(earlier, inbound[None, :], 0), axis=1)
    return arrived.reshape(peer_count * capacity, feature_count)[sender * capacity + offset_in]


def shards(student_query, key_cache, value_cache, grad_rows, out_weight, return_counts, block_sizes):
    counts = return_counts[0]
    me = lax.axis_index("seq")
    core = me % CORES
    side = me // CORES % SIDE // PAIR
    row_count, head_width = student_query.shape[1:]
    head_count = head_width // HEAD_DIM
    scale = HEAD_DIM ** -0.5
    peer_count = lax.axis_size("seq")
    clip_count = lax.axis_size("dp")
    local_rows = jnp.arange(row_count, dtype=jnp.int32)

    weight = lax.all_gather(out_weight, "dp", axis=0, tiled=True)

    (slots,) = call(
        functools.partial(pack_kernel, head_count),
        [((SLOTS, 3, row_count, HEAD_DIM), jnp.bfloat16)],
        "pack",
        1e6,
    )(student_query, key_cache, value_cache)
    inputs = trade(slots)
    own = inputs[:, 1:]
    far = send(own, dx=PAIR)
    beside = send(own, dcore=1)
    far_beside = send(far, dcore=1)

    packed, beside = lax.optimization_barrier((pack_rows(grad_rows[0], counts, me), beside))
    arrived = lax.all_to_all(packed, "seq", 0, 0, tiled=True)
    ordered = unpack_rows(arrived, counts, me, row_count)
    other_ordered = send(ordered, dcore=1)

    rank = jnp.arange(SLOTS, dtype=jnp.int32)

    def bases(which_side, which_core):
        return (((rank // PAIR) * SIDE + which_side * PAIR + rank % PAIR) * CORES + which_core) * row_count

    key_bases = jnp.concatenate(
        [bases(side, core), bases(side, 1 - core), bases(1 - side, core), bases(1 - side, 1 - core)]
    )
    places = (key_bases[:, None] + local_rows[None, :]).reshape(-1, KEY_SLOTS * row_count)
    positions = bases(side, core)[:, None] + local_rows[None, :]
    block_ends = jnp.cumsum(block_sizes[0])
    limits = jnp.min(
        jnp.where(block_ends > positions[:, :, None], block_ends, row_count * peer_count), axis=2
    )[:, :, None]

    column = ((SLOTS, row_count, 1), jnp.float32)
    wide = ((SLOTS, row_count, HEAD_DIM), jnp.float32)
    narrow = ((SLOTS, row_count, HEAD_DIM), jnp.bfloat16)
    carry = call(functools.partial(near_kernel, scale), [column, column, wide], "near", 4e9)(
        limits, places, inputs, own, beside
    )
    attended, exact, level = call(functools.partial(far_kernel, scale), [narrow, wide, column], "far", 4e9)(
        limits, places, inputs, far, far_beside, *carry
    )

    returned = trade(attended)
    share_heads = head_count // CORES
    own_part = lax.dynamic_slice_in_dim(returned, core * share_heads, share_heads, axis=0)
    other_part = send(
        lax.dynamic_slice_in_dim(returned, (1 - core) * share_heads, share_heads, axis=0), dcore=1
    )
    feature_count = ordered.shape[1]
    width = share_heads * HEAD_DIM
    (partial_sum,) = call(outer_kernel, [((width, feature_count), jnp.bfloat16)], "outer", 5e8)(
        own_part, other_part, ordered, other_ordered
    )
    chip_count = SIDE * SIDE
    share = width // chip_count
    cores_apart = [[chip * CORES + which for chip in range(chip_count)] for which in range(CORES)]
    pieces = lax.all_to_all(
        partial_sum.reshape(chip_count, share, feature_count), "seq", 0, 0, axis_index_groups=cores_apart, tiled=True
    )

    pieces, late_ordered = lax.optimization_barrier((pieces, ordered))
    (head_grad,) = call(functools.partial(project_kernel, head_count), [narrow], "project", 1e9)(late_ordered, weight)
    (clip_parts,) = call(
        sum_kernel, [((clip_count, share, feature_count // clip_count), jnp.bfloat16)], "sum", 1e6
    )(pieces)
    head_grad, clip_parts = lax.optimization_barrier((trade(head_grad), clip_parts))
    (grad_query,) = call(functools.partial(grad_kernel, scale), [narrow], "attend_grad", 1e10)(
        limits, places, inputs, head_grad, exact, level, own, beside, far, far_beside
    )
    grad_query = trade(grad_query)
    (grad_query_rows,) = call(
        functools.partial(join_kernel, head_count), [((1, row_count, head_width), jnp.bfloat16)], "join", 1e6
    )(grad_query)

    terms = lax.all_to_all(clip_parts, "dp", 0, 0, tiled=True)
    total = jnp.sum(terms.astype(jnp.float32), axis=0) / float(clip_count)
    total = lax.ppermute(
        total,
        "seq",
        [(chip * CORES + which, which * chip_count + chip) for chip in range(chip_count) for which in range(CORES)],
    )
    return (grad_query_rows, total)


def solution(mesh):
    in_specs = (
        P("dp", "seq", None),
        P("dp", "seq", None),
        P("dp", "seq", None),
        P("dp", "seq", None),
        P("dp", None),
        P("dp", None, None),
        P("dp", None),
    )
    out_specs = (P("dp", "seq", None), P("seq", "dp"))
    return jax.shard_map(shards, mesh=mesh, in_specs=in_specs, out_specs=out_specs, check_vma=False)
```

```python
import functools

import jax
import jax.numpy as jnp
from jax import lax
from jax.experimental import pallas as pl
from jax.experimental.pallas import tpu as pltpu
from jax.sharding import PartitionSpec as P

HEAD_DIM = 128
SIDE = 4
CORES = 2
PAIR = 2
SLOTS = SIDE * PAIR
QUERY_SLOTS = 2
KEY_SLOTS = 4
LOG2_E = 1.4426950408889634
HIDDEN = -1e30
LOWEST = -1e20
MIB = 1024 * 1024
NT = (((1,), (1,)), ((), ()))
NN = (((1,), (0,)), ((), ()))
TN = (((0,), (0,)), ((), ()))


def seat(y, x, core):
    return (y % SIDE * SIDE + x % SIDE) * CORES + core % CORES


def send(value, dx=0, dcore=0, flip=0):
    pairs = [
        (seat(y, x, core), seat(y, (x + dx) ^ flip, core + dcore))
        for y in range(SIDE)
        for x in range(SIDE)
        for core in range(CORES)
    ]
    return lax.ppermute(value, "seq", pairs)


def trade(slots, across=False):
    groups = [
        [
            seat(y, PAIR * step + fixed if across else PAIR * fixed + step, core)
            for y in range(SIDE)
            for step in range(PAIR)
        ]
        for fixed in range(PAIR)
        for core in range(CORES)
    ]
    return lax.all_to_all(slots, "seq", 0, 0, axis_index_groups=groups, tiled=True)


def tiles_of(refs):
    return [
        (ref.at[pl.ds(first, KEY_SLOTS), 0], ref.at[pl.ds(first, KEY_SLOTS), 1])
        for ref in refs
        for first in range(0, SLOTS, KEY_SLOTS)
    ]


def rows_of(ref):
    return ref[...].reshape(-1, HEAD_DIM)


def masked_keys(key_ref, hidden_ref, tile):
    rows = KEY_SLOTS * key_ref.shape[1]
    return jnp.concatenate([rows_of(key_ref), hidden_ref[pl.ds(tile * rows, rows), :]], axis=1)


def attend_blocks(scale, input_ref, member_ref, hidden_ref, tiles, start, finish):
    for block in range(SLOTS // QUERY_SLOTS):
        slots = pl.ds(block * QUERY_SLOTS, QUERY_SLOTS)
        query = jnp.concatenate([rows_of(input_ref.at[slots, 0]), rows_of(member_ref.at[slots])], axis=1)
        peak, total = start(slots, query.shape[0])
        for index, (key_ref, value_ref) in enumerate(tiles):
            keys = masked_keys(key_ref, hidden_ref, index)
            values = rows_of(value_ref)
            values = jnp.concatenate([values, jnp.ones_like(values)], axis=1)
            scores = lax.dot_general(query, keys, NT, preferred_element_type=jnp.float32)
            new_peak = jnp.maximum(peak, jnp.max(scores, axis=1, keepdims=True))
            rescale = jnp.exp2((peak - new_peak) * (scale * LOG2_E))
            weights = jnp.exp2((scores - new_peak) * (scale * LOG2_E)).astype(jnp.bfloat16)
            total = total * rescale + lax.dot_general(weights, values, NN, preferred_element_type=jnp.float32)
            peak = new_peak
        finish(block, slots, peak, total)


def split_rows(rows):
    return rows.reshape(QUERY_SLOTS, -1, rows.shape[1])


def near_kernel(scale, input_ref, member_ref, hidden_ref, own_ref, core_ref, peak_ref, total_ref):
    def start(slots, rows):
        return jnp.full((rows, 1), LOWEST, jnp.float32), jnp.zeros((rows, 2 * HEAD_DIM), jnp.float32)

    def finish(block, slots, peak, total):
        peak_ref[slots] = split_rows(peak)
        total_ref[slots] = split_rows(total)

    attend_blocks(scale, input_ref, member_ref, hidden_ref, tiles_of([own_ref, core_ref]), start, finish)


def far_kernel(
    scale, input_ref, member_ref, hidden_ref, own_ref, core_ref, peak_ref, total_ref, attended_ref, exact_ref, level_ref
):
    def start(slots, rows):
        return peak_ref[slots].reshape(rows, 1), total_ref[slots].reshape(rows, 2 * HEAD_DIM)

    def finish(block, slots, peak, total):
        norm = total[:, HEAD_DIM:]
        exact = total[:, :HEAD_DIM] / norm
        attended = split_rows(exact.astype(jnp.bfloat16))
        for pair in range(PAIR):
            attended_ref[block * PAIR + pair] = attended
        exact_ref[slots] = split_rows(exact)
        level_ref[slots] = split_rows(peak * (scale * LOG2_E) + jnp.log2(norm))

    tiles = tiles_of([own_ref, core_ref])
    attend_blocks(scale, input_ref, member_ref, hidden_ref, tiles, start, finish)


def grad_kernel(
    scale, input_ref, member_ref, hidden_ref, grad_ref, exact_ref, level_ref, own_ref, core_ref, far_ref, far_core_ref, out_ref
):
    tiles = tiles_of([own_ref, core_ref, far_ref, far_core_ref])
    for block in range(SLOTS // QUERY_SLOTS):
        slots = pl.ds(block * QUERY_SLOTS, QUERY_SLOTS)
        query = jnp.concatenate([rows_of(input_ref.at[slots, 0]), rows_of(member_ref.at[slots])], axis=1)
        level = rows_of(level_ref.at[slots])
        level = jnp.concatenate([level] * KEY_SLOTS, axis=1)
        grad = rows_of(grad_ref.at[slots])
        centre = jnp.sum(grad.astype(jnp.float32) * rows_of(exact_ref.at[slots]), axis=1, keepdims=True)
        total = jnp.zeros((query.shape[0], HEAD_DIM), jnp.float32)
        for index, (key_ref, value_ref) in enumerate(tiles):
            keys = masked_keys(key_ref, hidden_ref, index)
            scores = lax.dot_general(query, keys, NT, preferred_element_type=jnp.float32)
            probs = jnp.exp2(scores * (scale * LOG2_E) - level)
            grad_probs = lax.dot_general(grad, rows_of(value_ref), NT, preferred_element_type=jnp.float32)
            grad_scores = (probs * (grad_probs - centre)).astype(jnp.bfloat16)
            total = total + lax.dot_general(grad_scores, rows_of(key_ref), NN, preferred_element_type=jnp.float32)
        out_ref[slots] = split_rows((total * scale).astype(jnp.bfloat16))


def project_kernel(head_count, rows_ref, weight_ref, out_ref):
    rows = rows_ref[...]
    for slot in range(SLOTS):
        head = slot % head_count
        out_ref[slot] = lax.dot_general(
            rows, weight_ref[pl.ds(head * HEAD_DIM, HEAD_DIM), :], NT, preferred_element_type=jnp.float32
        ).astype(jnp.bfloat16)


def outer_kernel(head_count, parity_ref, own_ref, other_ref, *refs):
    row_refs, out_ref = refs[:-1], refs[-1]
    parity = parity_ref[0]
    rows = jnp.concatenate([ref[...] for ref in row_refs], axis=0)
    for head in range(head_count):
        attended = jnp.concatenate(
            [own_ref[head, parity], own_ref[head, 1 - parity], other_ref[head, parity], other_ref[head, 1 - parity]],
            axis=0,
        )
        term = lax.dot_general(attended, rows, TN, preferred_element_type=jnp.float32)
        out_ref[pl.ds(head * HEAD_DIM, HEAD_DIM), :] = term.astype(jnp.bfloat16)


def pack_kernel(head_count, query_ref, key_ref, value_ref, out_ref, sems):
    copies = []
    for slot in range(SLOTS):
        columns = pl.ds(slot % head_count * HEAD_DIM, HEAD_DIM)
        for place, ref in enumerate((query_ref, key_ref, value_ref)):
            copies.append(
                pltpu.make_async_copy(ref.at[0, :, columns], out_ref.at[slot, place], sems.at[slot, place])
            )
    for copy in copies:
        copy.start()
    for copy in copies:
        copy.wait()


def join_kernel(head_count, slots_ref, out_ref):
    for head in range(head_count):
        out_ref[0, :, pl.ds(head * HEAD_DIM, HEAD_DIM)] = slots_ref[head]


def sum_kernel(pieces_ref, out_ref):
    total = pieces_ref[0].astype(jnp.float32)
    for chip in range(1, pieces_ref.shape[0]):
        total = total + pieces_ref[chip].astype(jnp.float32)
    share, width = out_ref.shape[1:]
    across = total.shape[1] // width
    for clip in range(out_ref.shape[0]):
        row, column = clip // across * share, clip % across * width
        out_ref[clip] = total[row : row + share, column : column + width].astype(jnp.bfloat16)


def block_at(shape, *place):
    return pl.BlockSpec(shape, lambda step: place)


def call(kernel, out_shape, name, flops, scalars=0, **options):
    def run(*operands):
        spaces = [pl.BlockSpec(memory_space=pltpu.SMEM)] * scalars
        spaces = spaces + [pl.BlockSpec()] * (len(operands) - scalars)
        for place, spec in options.get("blocks", {}).items():
            spaces[place] = spec
        return pl.pallas_call(
            kernel,
            out_shape=[jax.ShapeDtypeStruct(shape, dtype) for shape, dtype in out_shape],
            grid=(1,) if "blocks" in options else (),
            in_specs=options.get("in_specs", spaces),
            out_specs=[pl.BlockSpec()] * len(out_shape),
            scratch_shapes=options.get("scratch_shapes", ()),
            compiler_params=pltpu.CompilerParams(vmem_limit_bytes=options.get("limit", 20) * MIB),
            cost_estimate=pl.CostEstimate(flops=int(flops), bytes_accessed=int(1e6), transcendentals=0),
            name=name,
        )(*operands)

    return run


def pack_rows(teacher_rows, counts, me):
    row_count = teacher_rows.shape[0]
    capacity = 2 * row_count // counts.shape[0]
    mine = lax.dynamic_index_in_dim(counts, me, 0, keepdims=False)
    starts = jnp.cumsum(mine) - mine
    slot = jnp.arange(capacity, dtype=jnp.int32)
    source_row = jnp.minimum(starts[:, None] + slot[None, :], row_count - 1)
    return teacher_rows[source_row]


def unpack_rows(arrived, counts, me, row_count):
    peer_count, capacity, feature_count = arrived.shape
    inbound = lax.dynamic_index_in_dim(counts, me, 1, keepdims=False)
    inbound_ends = jnp.cumsum(inbound)
    local_rows = jnp.arange(row_count, dtype=jnp.int32)
    earlier = inbound_ends[None, :] <= local_rows[:, None]
    sender = jnp.sum(earlier.astype(jnp.int32), axis=1)
    offset_in = local_rows - jnp.sum(jnp.where(earlier, inbound[None, :], 0), axis=1)
    return arrived.reshape(peer_count * capacity, feature_count)[sender * capacity + offset_in]


def shards(student_query, key_cache, value_cache, grad_rows, out_weight, return_counts, block_sizes):
    counts = return_counts[0]
    me = lax.axis_index("seq")
    core = me % CORES
    side = me // CORES % SIDE // PAIR
    row_count, head_width = student_query.shape[1:]
    head_count = head_width // HEAD_DIM
    scale = HEAD_DIM ** -0.5
    peer_count = lax.axis_size("seq")
    clip_count = lax.axis_size("dp")
    local_rows = jnp.arange(row_count, dtype=jnp.int32)

    weight = lax.all_gather(out_weight, "dp", axis=0, tiled=True)

    (slots,) = call(
        functools.partial(pack_kernel, head_count),
        [((SLOTS, 3, row_count, HEAD_DIM), jnp.bfloat16)],
        "pack",
        1e6,
        limit=56,
        in_specs=[pl.BlockSpec(memory_space=pl.ANY)] * 3,
        scratch_shapes=[pltpu.SemaphoreType.DMA((SLOTS, 3))],
    )(student_query, key_cache, value_cache)
    inputs = trade(slots)
    own = inputs[:, 1:]
    far = send(own, dx=PAIR)
    beside = send(own, dcore=1)

    rank = jnp.arange(SLOTS, dtype=jnp.int32)

    def bases(which_side, which_core):
        return (((rank // PAIR) * SIDE + which_side * PAIR + rank % PAIR) * CORES + which_core) * row_count

    key_bases = jnp.concatenate(
        [bases(side, core), bases(side, 1 - core), bases(1 - side, core), bases(1 - side, 1 - core)]
    )
    block_ends = jnp.cumsum(block_sizes[0])
    block_starts = block_ends - block_sizes[0]
    pad = HEAD_DIM - block_ends.shape[0]
    ends = jnp.pad(block_ends, (0, pad), constant_values=row_count * peer_count)
    starts = jnp.pad(block_starts, (0, pad), constant_values=row_count * peer_count)
    places = (key_bases[:, None] + local_rows[None, :]).reshape(-1, 1)
    hidden = jnp.where(places < ends[None, :], 0.0, HIDDEN).astype(jnp.bfloat16)
    positions = (bases(side, core)[:, None] + local_rows[None, :])[:, :, None]
    member = ((positions >= starts) & (positions < ends)).astype(jnp.bfloat16)

    column = ((SLOTS, row_count, 1), jnp.float32)
    double = ((SLOTS, row_count, 2 * HEAD_DIM), jnp.float32)
    wide = ((SLOTS, row_count, HEAD_DIM), jnp.float32)
    narrow = ((SLOTS, row_count, HEAD_DIM), jnp.bfloat16)
    pair_narrow = ((SLOTS, PAIR, row_count, HEAD_DIM), jnp.bfloat16)
    only_query = block_at((SLOTS, 1, row_count, HEAD_DIM), 0, 0, 0, 0)
    half_keys = (hidden.shape[0] // 2, HEAD_DIM)
    carry = call(
        functools.partial(near_kernel, scale),
        [column, double],
        "near",
        4e9,
        limit=56,
        blocks={0: only_query, 2: block_at(half_keys, 0, 0)},
    )(
        inputs, member, hidden, own, beside
    )
    packed, far, carry = lax.optimization_barrier((pack_rows(grad_rows[0], counts, me), far, carry))
    far_beside = send(far, dcore=1)
    arrived = lax.all_to_all(packed, "seq", 0, 0, tiled=True)
    attended, exact, level = call(
        functools.partial(far_kernel, scale),
        [pair_narrow, wide, wide],
        "far",
        4e9,
        limit=56,
        blocks={0: only_query, 2: block_at(half_keys, 1, 0)},
    )(
        inputs, member, hidden, far, far_beside, *carry
    )

    attended, arrived = lax.optimization_barrier((attended, arrived))
    ordered = unpack_rows(arrived, counts, me, row_count)
    parity = me // CORES % PAIR
    feature_count = ordered.shape[1]
    quarter = feature_count // (PAIR * CORES)

    def columns_for(which_parity, which_core):
        return lax.dynamic_slice(
            ordered, (0, (which_parity * CORES + which_core) * quarter), (row_count, quarter)
        )

    row_parts = (
        columns_for(parity, core),
        send(columns_for(1 - parity, core), flip=1),
        send(columns_for(parity, 1 - core), dcore=1),
        send(columns_for(1 - parity, 1 - core), flip=1, dcore=1),
    )
    returned = trade(attended)
    (partial_sum,) = call(
        functools.partial(outer_kernel, head_count), [((head_width, quarter), jnp.bfloat16)], "outer", 5e8, scalars=1
    )(parity.reshape(1), returned, send(returned[:head_count], dcore=1), *row_parts)
    pieces = trade(partial_sum.reshape(SLOTS, head_width // SLOTS, quarter), across=True)

    pieces, late_ordered = lax.optimization_barrier((pieces, ordered))
    (head_grad,) = call(functools.partial(project_kernel, head_count), [narrow], "project", 1e9, limit=56)(late_ordered, weight)
    (clip_parts,) = call(
        sum_kernel, [((clip_count, head_width // peer_count, feature_count // clip_count), jnp.bfloat16)], "sum", 1e6
    )(pieces)
    head_grad, clip_parts = lax.optimization_barrier((trade(head_grad), clip_parts))
    (grad_query,) = call(functools.partial(grad_kernel, scale), [narrow], "attend_grad", 1e10, limit=56, blocks={0: only_query})(
        inputs, member, hidden, head_grad, exact, level, own, beside, far, far_beside
    )
    grad_query = trade(grad_query)
    (grad_query_rows,) = call(
        functools.partial(join_kernel, head_count), [((1, row_count, head_width), jnp.bfloat16)], "join", 1e6
    )(grad_query)

    terms = lax.all_to_all(clip_parts, "dp", 0, 0, tiled=True)
    total = jnp.sum(terms.astype(jnp.float32), axis=0) / float(clip_count)
    across = quarter * clip_count // feature_count
    total = lax.ppermute(
        total,
        ("seq", "dp"),
        [
            (
                seat(y, PAIR * half + x, at) * clip_count + clip,
                seat(y, PAIR * half + clip // across // CORES, clip // across % CORES) * clip_count
                + (x * CORES + at) * across
                + clip % across,
            )
            for y in range(SIDE)
            for half in range(PAIR)
            for x in range(PAIR)
            for at in range(CORES)
            for clip in range(clip_count)
        ],
    )
    return (grad_query_rows, total)


def solution(mesh):
    in_specs = (
        P("dp", "seq", None),
        P("dp", "seq", None),
        P("dp", "seq", None),
        P("dp", "seq", None),
        P("dp", None),
        P("dp", None, None),
        P("dp", None),
    )
    out_specs = (P("dp", "seq", None), P("seq", "dp"))
    return jax.shard_map(shards, mesh=mesh, in_specs=in_specs, out_specs=out_specs, check_vma=False)
```

```python
import functools

import jax
import jax.numpy as jnp
from jax import lax
from jax.experimental import pallas as pl
from jax.experimental.pallas import tpu as pltpu
from jax.sharding import PartitionSpec as P

HEAD_DIM = 128
SIDE = 4
CORES = 2
PAIR = 2
SLOTS = SIDE * PAIR
QUERY_SLOTS = 2
KEY_SLOTS = 4
LOG2_E = 1.4426950408889634
HIDDEN = -1e30
LOWEST = -1e20
MIB = 1024 * 1024
NT = (((1,), (1,)), ((), ()))
NN = (((1,), (0,)), ((), ()))
TN = (((0,), (0,)), ((), ()))


def seat(y, x, core):
    return (y % SIDE * SIDE + x % SIDE) * CORES + core % CORES


def send(value, dx=0, dcore=0):
    pairs = [
        (seat(y, x, core), seat(y, x + dx, core + dcore))
        for y in range(SIDE)
        for x in range(SIDE)
        for core in range(CORES)
    ]
    return lax.ppermute(value, "seq", pairs)


def trade(slots):
    groups = [
        [seat(y, PAIR * side + x, core) for y in range(SIDE) for x in range(PAIR)]
        for side in range(PAIR)
        for core in range(CORES)
    ]
    return lax.all_to_all(slots, "seq", 0, 0, axis_index_groups=groups, tiled=True)


def holders():
    return [
        seat(head // PAIR, PAIR * side + head % PAIR, core)
        for head in range(SLOTS - PAIR)
        for side in range(PAIR)
        for core in range(CORES)
    ]


def place_blocks(block, me):
    held = holders()

    def pass_on(routes):
        return lax.ppermute(
            block, "seq", [(held[3 * turn + take], 4 * turn + put) for turn in range(len(held) // 3) for take, put in routes]
        )

    unit = block.shape[0] // 4
    first = pass_on([(0, 0), (1, 1), (2, 3)])
    second = pass_on([(0, 1), (2, 2)])
    third = pass_on([(1, 2)])
    kinds = [
        first[: 3 * unit],
        jnp.concatenate([second[3 * unit :], first[: 2 * unit]]),
        jnp.concatenate([third[2 * unit :], second[:unit]]),
        first[unit:],
    ]
    return lax.select_n(me % 4, *kinds)


def tiles_of(refs):
    return [
        (ref.at[pl.ds(first, KEY_SLOTS), 0], ref.at[pl.ds(first, KEY_SLOTS), 1])
        for ref in refs
        for first in range(0, SLOTS, KEY_SLOTS)
    ]


def rows_of(ref):
    return ref[...].reshape(-1, HEAD_DIM)


def masked_keys(key_ref, hidden_ref, tile):
    rows = KEY_SLOTS * key_ref.shape[1]
    return jnp.concatenate([rows_of(key_ref), hidden_ref[pl.ds(tile * rows, rows), :]], axis=1)


def attend_blocks(scale, input_ref, member_ref, hidden_ref, tiles, start, finish):
    for block in range(SLOTS // QUERY_SLOTS):
        slots = pl.ds(block * QUERY_SLOTS, QUERY_SLOTS)
        query = jnp.concatenate([rows_of(input_ref.at[slots, 0]), rows_of(member_ref.at[slots])], axis=1)
        peak, total = start(slots, query.shape[0])
        for index, (key_ref, value_ref) in enumerate(tiles):
            keys = masked_keys(key_ref, hidden_ref, index)
            values = rows_of(value_ref)
            values = jnp.concatenate([values, jnp.ones_like(values)], axis=1)
            scores = lax.dot_general(query, keys, NT, preferred_element_type=jnp.float32)
            new_peak = jnp.maximum(peak, jnp.max(scores, axis=1, keepdims=True))
            rescale = jnp.exp2((peak - new_peak) * (scale * LOG2_E))
            weights = jnp.exp2((scores - new_peak) * (scale * LOG2_E)).astype(jnp.bfloat16)
            total = total * rescale + lax.dot_general(weights, values, NN, preferred_element_type=jnp.float32)
            peak = new_peak
        finish(block, slots, peak, total)


def split_rows(rows):
    return rows.reshape(QUERY_SLOTS, -1, rows.shape[1])


def near_kernel(scale, input_ref, member_ref, hidden_ref, own_ref, core_ref, peak_ref, total_ref):
    def start(slots, rows):
        return jnp.full((rows, 1), LOWEST, jnp.float32), jnp.zeros((rows, 2 * HEAD_DIM), jnp.float32)

    def finish(block, slots, peak, total):
        peak_ref[slots] = split_rows(peak)
        total_ref[slots] = split_rows(total)

    attend_blocks(scale, input_ref, member_ref, hidden_ref, tiles_of([own_ref, core_ref]), start, finish)


def far_kernel(
    scale, input_ref, member_ref, hidden_ref, own_ref, core_ref, peak_ref, total_ref, attended_ref, exact_ref, level_ref
):
    def start(slots, rows):
        return peak_ref[slots].reshape(rows, 1), total_ref[slots].reshape(rows, 2 * HEAD_DIM)

    def finish(block, slots, peak, total):
        norm = total[:, HEAD_DIM:]
        exact = total[:, :HEAD_DIM] / norm
        attended_ref[slots] = split_rows(exact.astype(jnp.bfloat16))
        exact_ref[slots] = split_rows(exact)
        level_ref[slots] = split_rows(peak * (scale * LOG2_E) + jnp.log2(norm))

    tiles = tiles_of([own_ref, core_ref])
    attend_blocks(scale, input_ref, member_ref, hidden_ref, tiles, start, finish)


def grad_kernel(
    scale, input_ref, member_ref, hidden_ref, grad_ref, exact_ref, level_ref, own_ref, core_ref, far_ref, far_core_ref, out_ref
):
    tiles = tiles_of([own_ref, core_ref, far_ref, far_core_ref])
    for block in range(SLOTS // QUERY_SLOTS):
        slots = pl.ds(block * QUERY_SLOTS, QUERY_SLOTS)
        query = jnp.concatenate([rows_of(input_ref.at[slots, 0]), rows_of(member_ref.at[slots])], axis=1)
        level = rows_of(level_ref.at[slots])
        level = jnp.concatenate([level] * KEY_SLOTS, axis=1)
        grad = rows_of(grad_ref.at[slots])
        centre = jnp.sum(grad.astype(jnp.float32) * rows_of(exact_ref.at[slots]), axis=1, keepdims=True)
        total = jnp.zeros((query.shape[0], HEAD_DIM), jnp.float32)
        for index, (key_ref, value_ref) in enumerate(tiles):
            keys = masked_keys(key_ref, hidden_ref, index)
            scores = lax.dot_general(query, keys, NT, preferred_element_type=jnp.float32)
            probs = jnp.exp2(scores * (scale * LOG2_E) - level)
            grad_probs = lax.dot_general(grad, rows_of(value_ref), NT, preferred_element_type=jnp.float32)
            grad_scores = (probs * (grad_probs - centre)).astype(jnp.bfloat16)
            total = total + lax.dot_general(grad_scores, rows_of(key_ref), NN, preferred_element_type=jnp.float32)
        out_ref[slots] = split_rows((total * scale).astype(jnp.bfloat16))


def project_kernel(rows_ref, weight_ref, out_ref):
    weight = weight_ref[...]
    for slot in range(SLOTS):
        out_ref[slot] = lax.dot_general(rows_ref[slot], weight, NT, preferred_element_type=jnp.float32).astype(
            jnp.bfloat16
        )


def outer_kernel(attended_ref, rows_ref, out_ref):
    parts, share, feature_count = out_ref.shape
    attended = attended_ref[...].reshape(-1, HEAD_DIM)
    for first in range(0, feature_count, 4 * HEAD_DIM):
        columns = pl.ds(first, 4 * HEAD_DIM)
        rows = rows_ref[:, :, columns].reshape(attended.shape[0], -1)
        term = lax.dot_general(attended, rows, TN, preferred_element_type=jnp.float32).astype(jnp.bfloat16)
        out_ref[:, :, columns] = term.reshape(parts, share, -1)


def pack_kernel(head_count, query_ref, key_ref, value_ref, out_ref, sems):
    copies = []
    for slot in range(SLOTS):
        columns = pl.ds(slot % head_count * HEAD_DIM, HEAD_DIM)
        for place, ref in enumerate((query_ref, key_ref, value_ref)):
            copies.append(
                pltpu.make_async_copy(ref.at[0, :, columns], out_ref.at[slot, place], sems.at[slot, place])
            )
    for copy in copies:
        copy.start()
    for copy in copies:
        copy.wait()


def join_kernel(head_count, slots_ref, out_ref):
    for head in range(head_count):
        out_ref[0, :, pl.ds(head * HEAD_DIM, HEAD_DIM)] = slots_ref[head]


def sum_kernel(pieces_ref, out_ref):
    total = pieces_ref[0].astype(jnp.float32)
    for piece in range(1, pieces_ref.shape[0]):
        total = total + pieces_ref[piece].astype(jnp.float32)
    width = out_ref.shape[2]
    for clip in range(out_ref.shape[0]):
        out_ref[clip] = total[:, clip * width : (clip + 1) * width].astype(jnp.bfloat16)


def block_at(shape, *place):
    return pl.BlockSpec(shape, lambda step: place)


def call(kernel, out_shape, name, flops, scalars=0, **options):
    def run(*operands):
        spaces = [pl.BlockSpec(memory_space=pltpu.SMEM)] * scalars
        spaces = spaces + [pl.BlockSpec()] * (len(operands) - scalars)
        for place, spec in options.get("blocks", {}).items():
            spaces[place] = spec
        return pl.pallas_call(
            kernel,
            out_shape=[jax.ShapeDtypeStruct(shape, dtype) for shape, dtype in out_shape],
            grid=(1,) if "blocks" in options else (),
            in_specs=options.get("in_specs", spaces),
            out_specs=[pl.BlockSpec()] * len(out_shape),
            scratch_shapes=options.get("scratch_shapes", ()),
            compiler_params=pltpu.CompilerParams(vmem_limit_bytes=options.get("limit", 20) * MIB),
            cost_estimate=pl.CostEstimate(flops=int(flops), bytes_accessed=int(1e6), transcendentals=0),
            name=name,
        )(*operands)

    return run


def pack_rows(teacher_rows, counts, me):
    row_count = teacher_rows.shape[0]
    capacity = 2 * row_count // counts.shape[0]
    mine = lax.dynamic_index_in_dim(counts, me, 0, keepdims=False)
    starts = jnp.cumsum(mine) - mine
    slot = jnp.arange(capacity, dtype=jnp.int32)
    source_row = jnp.minimum(starts[:, None] + slot[None, :], row_count - 1)
    return teacher_rows[source_row]


def unpack_rows(arrived, counts, me, row_count):
    peer_count, capacity, feature_count = arrived.shape
    inbound = lax.dynamic_index_in_dim(counts, me, 1, keepdims=False)
    inbound_ends = jnp.cumsum(inbound)
    local_rows = jnp.arange(row_count, dtype=jnp.int32)
    earlier = inbound_ends[None, :] <= local_rows[:, None]
    sender = jnp.sum(earlier.astype(jnp.int32), axis=1)
    offset_in = local_rows - jnp.sum(jnp.where(earlier, inbound[None, :], 0), axis=1)
    return arrived.reshape(peer_count * capacity, feature_count)[sender * capacity + offset_in]


def shards(student_query, key_cache, value_cache, grad_rows, out_weight, return_counts, block_sizes):
    counts = return_counts[0]
    me = lax.axis_index("seq")
    core = me % CORES
    side = me // CORES % SIDE // PAIR
    row_count, head_width = student_query.shape[1:]
    head_count = head_width // HEAD_DIM
    scale = HEAD_DIM ** -0.5
    peer_count = lax.axis_size("seq")
    clip_count = lax.axis_size("dp")
    local_rows = jnp.arange(row_count, dtype=jnp.int32)

    weight = lax.all_gather(out_weight, "dp", axis=0, tiled=True)

    (slots,) = call(
        functools.partial(pack_kernel, head_count),
        [((SLOTS, 3, row_count, HEAD_DIM), jnp.bfloat16)],
        "pack",
        1e6,
        limit=56,
        in_specs=[pl.BlockSpec(memory_space=pl.ANY)] * 3,
        scratch_shapes=[pltpu.SemaphoreType.DMA((SLOTS, 3))],
    )(student_query, key_cache, value_cache)
    inputs = trade(slots)
    own = inputs[:, 1:]
    own, packed = lax.optimization_barrier((own, pack_rows(grad_rows[0], counts, me)))
    far = send(own, dx=PAIR)
    beside = send(own, dcore=1)
    packed, beside = lax.optimization_barrier((packed, beside))
    arrived = lax.all_to_all(packed, "seq", 0, 0, tiled=True)

    rank = jnp.arange(SLOTS, dtype=jnp.int32)

    def bases(which_side, which_core):
        return (((rank // PAIR) * SIDE + which_side * PAIR + rank % PAIR) * CORES + which_core) * row_count

    key_bases = jnp.concatenate(
        [bases(side, core), bases(side, 1 - core), bases(1 - side, core), bases(1 - side, 1 - core)]
    )
    block_ends = jnp.cumsum(block_sizes[0])
    block_starts = block_ends - block_sizes[0]
    pad = HEAD_DIM - block_ends.shape[0]
    ends = jnp.pad(block_ends, (0, pad), constant_values=row_count * peer_count)
    starts = jnp.pad(block_starts, (0, pad), constant_values=row_count * peer_count)
    places = (key_bases[:, None] + local_rows[None, :]).reshape(-1, 1)
    hidden = jnp.where(places < ends[None, :], 0.0, HIDDEN).astype(jnp.bfloat16)
    positions = (bases(side, core)[:, None] + local_rows[None, :])[:, :, None]
    member = ((positions >= starts) & (positions < ends)).astype(jnp.bfloat16)

    column = ((SLOTS, row_count, 1), jnp.float32)
    double = ((SLOTS, row_count, 2 * HEAD_DIM), jnp.float32)
    wide = ((SLOTS, row_count, HEAD_DIM), jnp.float32)
    narrow = ((SLOTS, row_count, HEAD_DIM), jnp.bfloat16)
    only_query = block_at((SLOTS, 1, row_count, HEAD_DIM), 0, 0, 0, 0)
    half_keys = (hidden.shape[0] // 2, HEAD_DIM)
    carry = call(
        functools.partial(near_kernel, scale),
        [column, double],
        "near",
        4e9,
        limit=56,
        blocks={0: only_query, 2: block_at(half_keys, 0, 0)},
    )(
        inputs, member, hidden, own, beside
    )
    far, carry = lax.optimization_barrier((far, carry))
    far_beside = send(far, dcore=1)
    ordered = unpack_rows(arrived, counts, me, row_count)
    copies = jnp.broadcast_to(ordered[None], (SLOTS,) + ordered.shape)
    far_beside, copies = lax.optimization_barrier((far_beside, copies))
    group_rows = trade(copies)
    attended, exact, level = call(
        functools.partial(far_kernel, scale),
        [narrow, wide, wide],
        "far",
        4e9,
        limit=56,
        blocks={0: only_query, 2: block_at(half_keys, 1, 0)},
    )(
        inputs, member, hidden, far, far_beside, *carry
    )

    feature_count = ordered.shape[1]
    parts = PAIR * CORES
    share = HEAD_DIM // parts
    (partial_sum,) = call(
        outer_kernel, [((parts, share, feature_count), jnp.bfloat16)], "outer", 1e9
    )(attended, group_rows)
    partners = [
        [seat(y, PAIR * side + x, at) for side in range(PAIR) for at in range(CORES)]
        for y in range(SIDE)
        for x in range(PAIR)
    ]
    pieces = lax.all_to_all(partial_sum, "seq", 0, 0, axis_index_groups=partners, tiled=True)

    slot = me // (SIDE * CORES) * PAIR + me // CORES % PAIR
    head_weight = lax.dynamic_slice_in_dim(weight, slot % head_count * HEAD_DIM, HEAD_DIM, axis=0)
    (head_grad,) = call(project_kernel, [narrow], "project", 1e9)(group_rows, head_weight)
    (grad_query,) = call(functools.partial(grad_kernel, scale), [narrow], "attend_grad", 1e10, limit=56, blocks={0: only_query})(
        inputs, member, hidden, head_grad, exact, level, own, beside, far, far_beside
    )
    grad_query = trade(grad_query)
    (grad_query_rows,) = call(
        functools.partial(join_kernel, head_count), [((1, row_count, head_width), jnp.bfloat16)], "join", 1e6
    )(grad_query)

    (clip_parts,) = call(
        sum_kernel, [((clip_count, share, feature_count // clip_count), jnp.bfloat16)], "sum", 1e6
    )(pieces)
    terms = lax.all_to_all(clip_parts, "dp", 0, 0, tiled=True)
    total = jnp.sum(terms.astype(jnp.float32), axis=0) / float(clip_count)
    total = place_blocks(total, me)
    return (grad_query_rows, total)


def solution(mesh):
    in_specs = (
        P("dp", "seq", None),
        P("dp", "seq", None),
        P("dp", "seq", None),
        P("dp", "seq", None),
        P("dp", None),
        P("dp", None, None),
        P("dp", None),
    )
    out_specs = (P("dp", "seq", None), P("seq", "dp"))
    return jax.shard_map(shards, mesh=mesh, in_specs=in_specs, out_specs=out_specs, check_vma=False)
```

```python
import functools

import jax
import jax.numpy as jnp
from jax import lax
from jax.experimental import pallas as pl
from jax.experimental.pallas import tpu as pltpu
from jax.sharding import PartitionSpec as P

HEAD_DIM = 128
SIDE = 4
CORES = 2
PAIR = 2
SLOTS = SIDE * PAIR
QUERY_SLOTS = 2
KEY_SLOTS = 8
LOG2_E = 1.4426950408889634
HIDDEN = -1e30
LOWEST = -1e20
MIB = 1024 * 1024
NT = (((1,), (1,)), ((), ()))
NN = (((1,), (0,)), ((), ()))
TN = (((0,), (0,)), ((), ()))


def seat(y, x, core):
    return (y % SIDE * SIDE + x % SIDE) * CORES + core % CORES


def send(value, dx=0, dcore=0):
    pairs = [
        (seat(y, x, core), seat(y, x + dx, core + dcore))
        for y in range(SIDE)
        for x in range(SIDE)
        for core in range(CORES)
    ]
    return lax.ppermute(value, "seq", pairs)


def trade(slots):
    groups = [
        [seat(y, PAIR * side + x, core) for y in range(SIDE) for x in range(PAIR)]
        for side in range(PAIR)
        for core in range(CORES)
    ]
    return lax.all_to_all(slots, "seq", 0, 0, axis_index_groups=groups, tiled=True)


def holders():
    return [
        seat(head // PAIR, PAIR * side + head % PAIR, core)
        for head in range(SLOTS - PAIR)
        for side in range(PAIR)
        for core in range(CORES)
    ]


def place_blocks(block, me):
    held = holders()

    def pass_on(routes):
        return lax.ppermute(
            block, "seq", [(held[3 * turn + take], 4 * turn + put) for turn in range(len(held) // 3) for take, put in routes]
        )

    unit = block.shape[0] // 4
    first = pass_on([(0, 0), (1, 1), (2, 3)])
    second = pass_on([(0, 1), (2, 2)])
    third = pass_on([(1, 2)])
    kinds = [
        first[: 3 * unit],
        jnp.concatenate([second[3 * unit :], first[: 2 * unit]]),
        jnp.concatenate([third[2 * unit :], second[:unit]]),
        first[unit:],
    ]
    return lax.select_n(me % 4, *kinds)


def tiles_of(refs):
    return [
        (ref.at[pl.ds(first, KEY_SLOTS), 0], ref.at[pl.ds(first, KEY_SLOTS), 1])
        for ref in refs
        for first in range(0, SLOTS, KEY_SLOTS)
    ]


def rows_of(ref):
    return ref[...].reshape(-1, HEAD_DIM)


def masked_keys(key_ref, hidden_ref, tile):
    rows = KEY_SLOTS * key_ref.shape[1]
    return jnp.concatenate([rows_of(key_ref), hidden_ref[pl.ds(tile * rows, rows), :]], axis=1)


def attend_blocks(scale, input_ref, member_ref, hidden_ref, tiles, start, finish):
    for block in range(SLOTS // QUERY_SLOTS):
        slots = pl.ds(block * QUERY_SLOTS, QUERY_SLOTS)
        query = jnp.concatenate([rows_of(input_ref.at[slots, 0]), rows_of(member_ref.at[slots])], axis=1)
        peak, total = start(slots, query.shape[0])
        for index, (key_ref, value_ref) in enumerate(tiles):
            keys = masked_keys(key_ref, hidden_ref, index)
            values = rows_of(value_ref)
            values = jnp.concatenate([values, jnp.ones_like(values)], axis=1)
            scores = lax.dot_general(query, keys, NT, preferred_element_type=jnp.float32)
            new_peak = jnp.maximum(peak, jnp.max(scores, axis=1, keepdims=True))
            rescale = jnp.exp2((peak - new_peak) * (scale * LOG2_E))
            weights = jnp.exp2((scores - new_peak) * (scale * LOG2_E)).astype(jnp.bfloat16)
            total = total * rescale + lax.dot_general(weights, values, NN, preferred_element_type=jnp.float32)
            peak = new_peak
        finish(block, slots, peak, total)


def split_rows(rows):
    return rows.reshape(QUERY_SLOTS, -1, rows.shape[1])


def near_kernel(scale, input_ref, member_ref, hidden_ref, own_ref, core_ref, peak_ref, total_ref):
    def start(slots, rows):
        return jnp.full((rows, 1), LOWEST, jnp.float32), jnp.zeros((rows, 2 * HEAD_DIM), jnp.float32)

    def finish(block, slots, peak, total):
        peak_ref[slots] = split_rows(peak)
        total_ref[slots] = split_rows(total)

    attend_blocks(scale, input_ref, member_ref, hidden_ref, tiles_of([own_ref, core_ref]), start, finish)


def far_kernel(
    scale, input_ref, member_ref, hidden_ref, own_ref, core_ref, peak_ref, total_ref, attended_ref, exact_ref, level_ref
):
    def start(slots, rows):
        return peak_ref[slots].reshape(rows, 1), total_ref[slots].reshape(rows, 2 * HEAD_DIM)

    def finish(block, slots, peak, total):
        norm = total[:, HEAD_DIM:]
        exact = total[:, :HEAD_DIM] / norm
        attended_ref[slots] = split_rows(exact.astype(jnp.bfloat16))
        exact_ref[slots] = split_rows(exact)
        level_ref[slots] = split_rows(peak * (scale * LOG2_E) + jnp.log2(norm))

    tiles = tiles_of([own_ref, core_ref])
    attend_blocks(scale, input_ref, member_ref, hidden_ref, tiles, start, finish)


def grad_kernel(
    scale, input_ref, member_ref, hidden_ref, grad_ref, exact_ref, level_ref, own_ref, core_ref, far_ref, far_core_ref, out_ref
):
    tiles = tiles_of([own_ref, core_ref, far_ref, far_core_ref])
    for block in range(SLOTS // QUERY_SLOTS):
        slots = pl.ds(block * QUERY_SLOTS, QUERY_SLOTS)
        query = jnp.concatenate([rows_of(input_ref.at[slots, 0]), rows_of(member_ref.at[slots])], axis=1)
        level = rows_of(level_ref.at[slots])
        level = jnp.concatenate([level] * KEY_SLOTS, axis=1)
        grad = rows_of(grad_ref.at[slots])
        centre = jnp.sum(grad.astype(jnp.float32) * rows_of(exact_ref.at[slots]), axis=1, keepdims=True)
        total = jnp.zeros((query.shape[0], HEAD_DIM), jnp.float32)
        for index, (key_ref, value_ref) in enumerate(tiles):
            keys = masked_keys(key_ref, hidden_ref, index)
            scores = lax.dot_general(query, keys, NT, preferred_element_type=jnp.float32)
            probs = jnp.exp2(scores * (scale * LOG2_E) - level)
            grad_probs = lax.dot_general(grad, rows_of(value_ref), NT, preferred_element_type=jnp.float32)
            grad_scores = (probs * (grad_probs - centre)).astype(jnp.bfloat16)
            total = total + lax.dot_general(grad_scores, rows_of(key_ref), NN, preferred_element_type=jnp.float32)
        out_ref[slots] = split_rows((total * scale).astype(jnp.bfloat16))


def project_kernel(rows_ref, weight_ref, out_ref):
    weight = weight_ref[...]
    for slot in range(SLOTS):
        out_ref[slot] = lax.dot_general(rows_ref[slot], weight, NT, preferred_element_type=jnp.float32).astype(
            jnp.bfloat16
        )


def outer_kernel(attended_ref, rows_ref, out_ref):
    parts, share, feature_count = out_ref.shape
    attended = attended_ref[...].reshape(-1, HEAD_DIM)
    for first in range(0, feature_count, 4 * HEAD_DIM):
        columns = pl.ds(first, 4 * HEAD_DIM)
        rows = rows_ref[:, :, columns].reshape(attended.shape[0], -1)
        term = lax.dot_general(attended, rows, TN, preferred_element_type=jnp.float32).astype(jnp.bfloat16)
        out_ref[:, :, columns] = term.reshape(parts, share, -1)


def pack_kernel(head_count, query_ref, key_ref, value_ref, out_ref, sems):
    copies = []
    for slot in range(SLOTS):
        columns = pl.ds(slot % head_count * HEAD_DIM, HEAD_DIM)
        for place, ref in enumerate((query_ref, key_ref, value_ref)):
            copies.append(
                pltpu.make_async_copy(ref.at[0, :, columns], out_ref.at[slot, place], sems.at[slot, place])
            )
    for copy in copies:
        copy.start()
    for copy in copies:
        copy.wait()


def join_kernel(head_count, slots_ref, out_ref):
    for head in range(head_count):
        out_ref[0, :, pl.ds(head * HEAD_DIM, HEAD_DIM)] = slots_ref[head]


def sum_kernel(pieces_ref, out_ref):
    total = pieces_ref[0].astype(jnp.float32)
    for piece in range(1, pieces_ref.shape[0]):
        total = total + pieces_ref[piece].astype(jnp.float32)
    width = out_ref.shape[2]
    for clip in range(out_ref.shape[0]):
        out_ref[clip] = total[:, clip * width : (clip + 1) * width].astype(jnp.bfloat16)


def block_at(shape, *place):
    return pl.BlockSpec(shape, lambda step: place)


def call(kernel, out_shape, name, flops, scalars=0, **options):
    def run(*operands):
        spaces = [pl.BlockSpec(memory_space=pltpu.SMEM)] * scalars
        spaces = spaces + [pl.BlockSpec()] * (len(operands) - scalars)
        for place, spec in options.get("blocks", {}).items():
            spaces[place] = spec
        return pl.pallas_call(
            kernel,
            out_shape=[jax.ShapeDtypeStruct(shape, dtype) for shape, dtype in out_shape],
            grid=(1,) if "blocks" in options else (),
            in_specs=options.get("in_specs", spaces),
            out_specs=[pl.BlockSpec()] * len(out_shape),
            scratch_shapes=options.get("scratch_shapes", ()),
            compiler_params=pltpu.CompilerParams(vmem_limit_bytes=options.get("limit", 20) * MIB),
            cost_estimate=pl.CostEstimate(flops=int(flops), bytes_accessed=int(1e6), transcendentals=0),
            name=name,
        )(*operands)

    return run


def pack_rows(teacher_rows, counts, me):
    row_count = teacher_rows.shape[0]
    capacity = 2 * row_count // counts.shape[0]
    mine = lax.dynamic_index_in_dim(counts, me, 0, keepdims=False)
    starts = jnp.cumsum(mine) - mine
    slot = jnp.arange(capacity, dtype=jnp.int32)
    source_row = jnp.minimum(starts[:, None] + slot[None, :], row_count - 1)
    return teacher_rows[source_row]


def unpack_rows(arrived, counts, me, row_count):
    peer_count, capacity, feature_count = arrived.shape
    inbound = lax.dynamic_index_in_dim(counts, me, 1, keepdims=False)
    inbound_ends = jnp.cumsum(inbound)
    local_rows = jnp.arange(row_count, dtype=jnp.int32)
    earlier = inbound_ends[None, :] <= local_rows[:, None]
    sender = jnp.sum(earlier.astype(jnp.int32), axis=1)
    offset_in = local_rows - jnp.sum(jnp.where(earlier, inbound[None, :], 0), axis=1)
    return arrived.reshape(peer_count * capacity, feature_count)[sender * capacity + offset_in]


def shards(student_query, key_cache, value_cache, grad_rows, out_weight, return_counts, block_sizes):
    counts = return_counts[0]
    me = lax.axis_index("seq")
    core = me % CORES
    side = me // CORES % SIDE // PAIR
    row_count, head_width = student_query.shape[1:]
    head_count = head_width // HEAD_DIM
    scale = HEAD_DIM ** -0.5
    peer_count = lax.axis_size("seq")
    clip_count = lax.axis_size("dp")
    local_rows = jnp.arange(row_count, dtype=jnp.int32)

    weight = lax.all_gather(out_weight, "dp", axis=0, tiled=True)

    (slots,) = call(
        functools.partial(pack_kernel, head_count),
        [((SLOTS, 3, row_count, HEAD_DIM), jnp.bfloat16)],
        "pack",
        1e6,
        limit=56,
        in_specs=[pl.BlockSpec(memory_space=pl.ANY)] * 3,
        scratch_shapes=[pltpu.SemaphoreType.DMA((SLOTS, 3))],
    )(student_query, key_cache, value_cache)
    inputs = trade(slots)
    inputs, packed = lax.optimization_barrier((inputs, pack_rows(grad_rows[0], counts, me)))
    own = inputs[:, 1:]
    arrived = lax.all_to_all(packed, "seq", 0, 0, tiled=True)
    beside = send(own, dcore=1)

    rank = jnp.arange(SLOTS, dtype=jnp.int32)

    def bases(which_side, which_core):
        return (((rank // PAIR) * SIDE + which_side * PAIR + rank % PAIR) * CORES + which_core) * row_count

    key_bases = jnp.concatenate(
        [bases(side, core), bases(side, 1 - core), bases(1 - side, core), bases(1 - side, 1 - core)]
    )
    block_ends = jnp.cumsum(block_sizes[0])
    block_starts = block_ends - block_sizes[0]
    pad = HEAD_DIM - block_ends.shape[0]
    ends = jnp.pad(block_ends, (0, pad), constant_values=row_count * peer_count)
    starts = jnp.pad(block_starts, (0, pad), constant_values=row_count * peer_count)
    places = (key_bases[:, None] + local_rows[None, :]).reshape(-1, 1)
    hidden = jnp.where(places < ends[None, :], 0.0, HIDDEN).astype(jnp.bfloat16)
    positions = (bases(side, core)[:, None] + local_rows[None, :])[:, :, None]
    member = ((positions >= starts) & (positions < ends)).astype(jnp.bfloat16)

    column = ((SLOTS, row_count, 1), jnp.float32)
    double = ((SLOTS, row_count, 2 * HEAD_DIM), jnp.float32)
    wide = ((SLOTS, row_count, HEAD_DIM), jnp.float32)
    narrow = ((SLOTS, row_count, HEAD_DIM), jnp.bfloat16)
    only_query = block_at((SLOTS, 1, row_count, HEAD_DIM), 0, 0, 0, 0)
    half_keys = (hidden.shape[0] // 2, HEAD_DIM)
    carry = call(
        functools.partial(near_kernel, scale),
        [column, double],
        "near",
        4e9,
        limit=56,
        blocks={0: only_query, 2: block_at(half_keys, 0, 0)},
    )(
        inputs, member, hidden, own, beside
    )
    ordered = unpack_rows(arrived, counts, me, row_count)
    copies = jnp.broadcast_to(ordered[None], (SLOTS,) + ordered.shape)
    late_own, copies, carry = lax.optimization_barrier((own, copies, carry))
    far = send(late_own, dx=PAIR)
    group_rows = trade(copies)
    far_beside = send(far, dcore=1)
    attended, exact, level = call(
        functools.partial(far_kernel, scale),
        [narrow, wide, wide],
        "far",
        4e9,
        limit=56,
        blocks={0: only_query, 2: block_at(half_keys, 1, 0)},
    )(
        inputs, member, hidden, far, far_beside, *carry
    )

    feature_count = ordered.shape[1]
    parts = PAIR * CORES
    share = HEAD_DIM // parts
    (partial_sum,) = call(
        outer_kernel, [((parts, share, feature_count), jnp.bfloat16)], "outer", 1e9
    )(attended, group_rows)
    partners = [
        [seat(y, PAIR * side + x, at) for side in range(PAIR) for at in range(CORES)]
        for y in range(SIDE)
        for x in range(PAIR)
    ]
    pieces = lax.all_to_all(partial_sum, "seq", 0, 0, axis_index_groups=partners, tiled=True)

    slot = me // (SIDE * CORES) * PAIR + me // CORES % PAIR
    head_weight = lax.dynamic_slice_in_dim(weight, slot % head_count * HEAD_DIM, HEAD_DIM, axis=0)
    (head_grad,) = call(project_kernel, [narrow], "project", 1e9)(group_rows, head_weight)
    (grad_query,) = call(functools.partial(grad_kernel, scale), [narrow], "attend_grad", 1e10, limit=56, blocks={0: only_query})(
        inputs, member, hidden, head_grad, exact, level, own, beside, far, far_beside
    )
    pieces, grad_query = lax.optimization_barrier((pieces, grad_query))
    (clip_parts,) = call(
        sum_kernel, [((clip_count, share, feature_count // clip_count), jnp.bfloat16)], "sum", 1e6
    )(pieces)
    terms = lax.all_to_all(clip_parts, "dp", 0, 0, tiled=True)
    total = jnp.sum(terms.astype(jnp.float32), axis=0) / float(clip_count)
    total, grad_query = lax.optimization_barrier((total, grad_query))
    total = place_blocks(total, me)
    grad_query = trade(grad_query)
    (grad_query_rows,) = call(
        functools.partial(join_kernel, head_count), [((1, row_count, head_width), jnp.bfloat16)], "join", 1e6
    )(grad_query)
    return (grad_query_rows, total)


def solution(mesh):
    in_specs = (
        P("dp", "seq", None),
        P("dp", "seq", None),
        P("dp", "seq", None),
        P("dp", "seq", None),
        P("dp", None),
        P("dp", None, None),
        P("dp", None),
    )
    out_specs = (P("dp", "seq", None), P("seq", "dp"))
    return jax.shard_map(shards, mesh=mesh, in_specs=in_specs, out_specs=out_specs, check_vma=False)
```

```python
import functools

import jax
import jax.numpy as jnp
from jax import lax
from jax.experimental import pallas as pl
from jax.experimental.pallas import tpu as pltpu
from jax.sharding import PartitionSpec as P

HEAD_DIM = 128
SIDE = 4
CORES = 2
PAIR = 2
SLOTS = SIDE * PAIR
QUERY_SLOTS = 2
KEY_SLOTS = 8
LOG2_E = 1.4426950408889634
HIDDEN = -1e30
LOWEST = -1e20
MIB = 1024 * 1024
NT = (((1,), (1,)), ((), ()))
NN = (((1,), (0,)), ((), ()))
TN = (((0,), (0,)), ((), ()))


def seat(y, x, core):
    return (y % SIDE * SIDE + x % SIDE) * CORES + core % CORES


def column_of(side, step):
    return step if side == 0 else SIDE - 1 - step


def send(value, mirror=False, dcore=0):
    pairs = [
        (seat(y, x, core), seat(y, SIDE - 1 - x if mirror else x, core + dcore))
        for y in range(SIDE)
        for x in range(SIDE)
        for core in range(CORES)
    ]
    return lax.ppermute(value, "seq", pairs)


def trade(slots):
    groups = [
        [seat(y, column_of(side, step), core) for y in range(SIDE) for step in range(PAIR)]
        for side in range(PAIR)
        for core in range(CORES)
    ]
    return lax.all_to_all(slots, "seq", 0, 0, axis_index_groups=groups, tiled=True)


def holders():
    return [
        seat(head // PAIR, column_of(side, head % PAIR), core)
        for head in range(SLOTS - PAIR)
        for side in range(PAIR)
        for core in range(CORES)
    ]


def place_blocks(block, me):
    held = holders()

    def pass_on(routes):
        return lax.ppermute(
            block, "seq", [(held[3 * turn + take], 4 * turn + put) for turn in range(len(held) // 3) for take, put in routes]
        )

    unit = block.shape[0] // 4
    first = pass_on([(0, 0), (1, 1), (2, 3)])
    second = pass_on([(0, 1), (2, 2)])
    third = pass_on([(1, 2)])
    kinds = [
        first[: 3 * unit],
        jnp.concatenate([second[3 * unit :], first[: 2 * unit]]),
        jnp.concatenate([third[2 * unit :], second[:unit]]),
        first[unit:],
    ]
    return lax.select_n(me % 4, *kinds)


def tiles_of(refs):
    return [
        (ref.at[pl.ds(first, KEY_SLOTS), 0], ref.at[pl.ds(first, KEY_SLOTS), 1])
        for ref in refs
        for first in range(0, SLOTS, KEY_SLOTS)
    ]


def rows_of(ref):
    return ref[...].reshape(-1, HEAD_DIM)


def masked_keys(key_ref, hidden_ref, tile):
    rows = KEY_SLOTS * key_ref.shape[1]
    return jnp.concatenate([rows_of(key_ref), hidden_ref[pl.ds(tile * rows, rows), :]], axis=1)


def attend_blocks(scale, input_ref, member_ref, hidden_ref, tiles, start, finish):
    for block in range(SLOTS // QUERY_SLOTS):
        slots = pl.ds(block * QUERY_SLOTS, QUERY_SLOTS)
        query = jnp.concatenate([rows_of(input_ref.at[slots, 0]), rows_of(member_ref.at[slots])], axis=1)
        peak, total = start(slots, query.shape[0])
        for index, (key_ref, value_ref) in enumerate(tiles):
            keys = masked_keys(key_ref, hidden_ref, index)
            values = rows_of(value_ref)
            values = jnp.concatenate([values, jnp.ones_like(values)], axis=1)
            scores = lax.dot_general(query, keys, NT, preferred_element_type=jnp.float32)
            new_peak = jnp.maximum(peak, jnp.max(scores, axis=1, keepdims=True))
            rescale = jnp.exp2((peak - new_peak) * (scale * LOG2_E))
            weights = jnp.exp2((scores - new_peak) * (scale * LOG2_E)).astype(jnp.bfloat16)
            total = total * rescale + lax.dot_general(weights, values, NN, preferred_element_type=jnp.float32)
            peak = new_peak
        finish(block, slots, peak, total)


def split_rows(rows):
    return rows.reshape(QUERY_SLOTS, -1, rows.shape[1])


def near_kernel(scale, input_ref, member_ref, hidden_ref, own_ref, core_ref, peak_ref, total_ref):
    def start(slots, rows):
        return jnp.full((rows, 1), LOWEST, jnp.float32), jnp.zeros((rows, 2 * HEAD_DIM), jnp.float32)

    def finish(block, slots, peak, total):
        peak_ref[slots] = split_rows(peak)
        total_ref[slots] = split_rows(total)

    attend_blocks(scale, input_ref, member_ref, hidden_ref, tiles_of([own_ref, core_ref]), start, finish)


def far_kernel(
    scale, input_ref, member_ref, hidden_ref, own_ref, core_ref, peak_ref, total_ref, attended_ref, exact_ref, level_ref
):
    def start(slots, rows):
        return peak_ref[slots].reshape(rows, 1), total_ref[slots].reshape(rows, 2 * HEAD_DIM)

    def finish(block, slots, peak, total):
        norm = total[:, HEAD_DIM:]
        exact = total[:, :HEAD_DIM] / norm
        attended_ref[slots] = split_rows(exact.astype(jnp.bfloat16))
        exact_ref[slots] = split_rows(exact)
        level_ref[slots] = split_rows(peak * (scale * LOG2_E) + jnp.log2(norm))

    tiles = tiles_of([own_ref, core_ref])
    attend_blocks(scale, input_ref, member_ref, hidden_ref, tiles, start, finish)


def grad_kernel(
    scale, blocks, input_ref, member_ref, hidden_ref, grad_ref, exact_ref, level_ref, own_ref, core_ref, far_ref, far_core_ref, *out_refs
):
    out_ref = out_refs[-1]
    for early_ref in out_refs[:-1]:
        out_ref[pl.ds(0, early_ref.shape[0])] = early_ref[...]
    tiles = tiles_of([own_ref, core_ref, far_ref, far_core_ref])
    for block in blocks:
        slots = pl.ds(block * QUERY_SLOTS, QUERY_SLOTS)
        query = jnp.concatenate([rows_of(input_ref.at[slots, 0]), rows_of(member_ref.at[slots])], axis=1)
        level = rows_of(level_ref.at[slots])
        level = jnp.concatenate([level] * KEY_SLOTS, axis=1)
        grad = rows_of(grad_ref.at[slots])
        centre = jnp.sum(grad.astype(jnp.float32) * rows_of(exact_ref.at[slots]), axis=1, keepdims=True)
        total = jnp.zeros((query.shape[0], HEAD_DIM), jnp.float32)
        for index, (key_ref, value_ref) in enumerate(tiles):
            keys = masked_keys(key_ref, hidden_ref, index)
            scores = lax.dot_general(query, keys, NT, preferred_element_type=jnp.float32)
            probs = jnp.exp2(scores * (scale * LOG2_E) - level)
            grad_probs = lax.dot_general(grad, rows_of(value_ref), NT, preferred_element_type=jnp.float32)
            grad_scores = (probs * (grad_probs - centre)).astype(jnp.bfloat16)
            total = total + lax.dot_general(grad_scores, rows_of(key_ref), NN, preferred_element_type=jnp.float32)
        out_ref[slots] = split_rows((total * scale).astype(jnp.bfloat16))


def project_kernel(rows_ref, weight_ref, out_ref):
    weight = weight_ref[...]
    for slot in range(SLOTS):
        out_ref[slot] = lax.dot_general(rows_ref[slot], weight, NT, preferred_element_type=jnp.float32).astype(
            jnp.bfloat16
        )


def outer_kernel(attended_ref, rows_ref, out_ref):
    parts, share, feature_count = out_ref.shape
    attended = attended_ref[...].reshape(-1, HEAD_DIM)
    for first in range(0, feature_count, 4 * HEAD_DIM):
        columns = pl.ds(first, 4 * HEAD_DIM)
        rows = rows_ref[:, :, columns].reshape(attended.shape[0], -1)
        term = lax.dot_general(attended, rows, TN, preferred_element_type=jnp.float32).astype(jnp.bfloat16)
        out_ref[:, :, columns] = term.reshape(parts, share, -1)


def pack_kernel(head_count, query_ref, key_ref, value_ref, out_ref, sems):
    copies = []
    for slot in range(SLOTS):
        columns = pl.ds(slot % head_count * HEAD_DIM, HEAD_DIM)
        for place, ref in enumerate((query_ref, key_ref, value_ref)):
            copies.append(
                pltpu.make_async_copy(ref.at[0, :, columns], out_ref.at[slot, place], sems.at[slot, place])
            )
    for copy in copies:
        copy.start()
    for copy in copies:
        copy.wait()


def join_kernel(head_count, slots_ref, out_ref):
    for head in range(head_count):
        out_ref[0, :, pl.ds(head * HEAD_DIM, HEAD_DIM)] = slots_ref[head]


def sum_kernel(pieces_ref, out_ref):
    total = pieces_ref[0].astype(jnp.float32)
    for piece in range(1, pieces_ref.shape[0]):
        total = total + pieces_ref[piece].astype(jnp.float32)
    width = out_ref.shape[2]
    for clip in range(out_ref.shape[0]):
        out_ref[clip] = total[:, clip * width : (clip + 1) * width].astype(jnp.bfloat16)


def block_at(shape, *place):
    return pl.BlockSpec(shape, lambda step: place)


def call(kernel, out_shape, name, flops, scalars=0, **options):
    def run(*operands):
        spaces = [pl.BlockSpec(memory_space=pltpu.SMEM)] * scalars
        spaces = spaces + [pl.BlockSpec()] * (len(operands) - scalars)
        for place, spec in options.get("blocks", {}).items():
            spaces[place] = spec
        return pl.pallas_call(
            kernel,
            out_shape=[jax.ShapeDtypeStruct(shape, dtype) for shape, dtype in out_shape],
            grid=(1,) if "blocks" in options else (),
            in_specs=options.get("in_specs", spaces),
            out_specs=[pl.BlockSpec()] * len(out_shape),
            scratch_shapes=options.get("scratch_shapes", ()),
            compiler_params=pltpu.CompilerParams(vmem_limit_bytes=options.get("limit", 20) * MIB),
            cost_estimate=pl.CostEstimate(flops=int(flops), bytes_accessed=int(1e6), transcendentals=0),
            name=name,
        )(*operands)

    return run


def pack_rows(teacher_rows, counts, me):
    row_count = teacher_rows.shape[0]
    capacity = 2 * row_count // counts.shape[0]
    mine = lax.dynamic_index_in_dim(counts, me, 0, keepdims=False)
    starts = jnp.cumsum(mine) - mine
    slot = jnp.arange(capacity, dtype=jnp.int32)
    source_row = jnp.minimum(starts[:, None] + slot[None, :], row_count - 1)
    return teacher_rows[source_row]


def unpack_rows(arrived, counts, me, row_count):
    peer_count, capacity, feature_count = arrived.shape
    inbound = lax.dynamic_index_in_dim(counts, me, 1, keepdims=False)
    inbound_ends = jnp.cumsum(inbound)
    local_rows = jnp.arange(row_count, dtype=jnp.int32)
    earlier = inbound_ends[None, :] <= local_rows[:, None]
    sender = jnp.sum(earlier.astype(jnp.int32), axis=1)
    offset_in = local_rows - jnp.sum(jnp.where(earlier, inbound[None, :], 0), axis=1)
    return arrived.reshape(peer_count * capacity, feature_count)[sender * capacity + offset_in]


def shards(student_query, key_cache, value_cache, grad_rows, out_weight, return_counts, block_sizes):
    counts = return_counts[0]
    me = lax.axis_index("seq")
    core = me % CORES
    side = me // CORES % SIDE // PAIR
    row_count, head_width = student_query.shape[1:]
    head_count = head_width // HEAD_DIM
    scale = HEAD_DIM ** -0.5
    peer_count = lax.axis_size("seq")
    clip_count = lax.axis_size("dp")
    local_rows = jnp.arange(row_count, dtype=jnp.int32)

    weight = lax.all_gather(out_weight, "dp", axis=0, tiled=True)

    (slots,) = call(
        functools.partial(pack_kernel, head_count),
        [((SLOTS, 3, row_count, HEAD_DIM), jnp.bfloat16)],
        "pack",
        1e6,
        limit=56,
        in_specs=[pl.BlockSpec(memory_space=pl.ANY)] * 3,
        scratch_shapes=[pltpu.SemaphoreType.DMA((SLOTS, 3))],
    )(student_query, key_cache, value_cache)
    inputs = trade(slots)
    inputs, packed = lax.optimization_barrier((inputs, pack_rows(grad_rows[0], counts, me)))
    own = inputs[:, 1:]
    arrived = lax.all_to_all(packed, "seq", 0, 0, tiled=True)
    beside = send(own, dcore=1)

    rank = jnp.arange(SLOTS, dtype=jnp.int32)

    def bases(which_side, which_core):
        column = which_side * (SIDE - 1) + (1 - 2 * which_side) * (rank % PAIR)
        return (((rank // PAIR) * SIDE + column) * CORES + which_core) * row_count

    key_bases = jnp.concatenate(
        [bases(side, core), bases(side, 1 - core), bases(1 - side, core), bases(1 - side, 1 - core)]
    )
    block_ends = jnp.cumsum(block_sizes[0])
    block_starts = block_ends - block_sizes[0]
    pad = HEAD_DIM - block_ends.shape[0]
    ends = jnp.pad(block_ends, (0, pad), constant_values=row_count * peer_count)
    starts = jnp.pad(block_starts, (0, pad), constant_values=row_count * peer_count)
    places = (key_bases[:, None] + local_rows[None, :]).reshape(-1, 1)
    hidden = jnp.where(places < ends[None, :], 0.0, HIDDEN).astype(jnp.bfloat16)
    positions = (bases(side, core)[:, None] + local_rows[None, :])[:, :, None]
    member = ((positions >= starts) & (positions < ends)).astype(jnp.bfloat16)

    column = ((SLOTS, row_count, 1), jnp.float32)
    double = ((SLOTS, row_count, 2 * HEAD_DIM), jnp.float32)
    wide = ((SLOTS, row_count, HEAD_DIM), jnp.float32)
    narrow = ((SLOTS, row_count, HEAD_DIM), jnp.bfloat16)
    only_query = block_at((SLOTS, 1, row_count, HEAD_DIM), 0, 0, 0, 0)
    half_keys = (hidden.shape[0] // 2, HEAD_DIM)
    carry = call(
        functools.partial(near_kernel, scale),
        [column, double],
        "near",
        4e9,
        limit=56,
        blocks={0: only_query, 2: block_at(half_keys, 0, 0)},
    )(
        inputs, member, hidden, own, beside
    )
    ordered = unpack_rows(arrived, counts, me, row_count)
    copies = jnp.broadcast_to(ordered[None], (SLOTS,) + ordered.shape)
    late_own, copies, carry = lax.optimization_barrier((own, copies, carry))
    group_rows = trade(copies)
    far = send(late_own, mirror=True)
    far_beside = send(far, dcore=1)
    attended, exact, level = call(
        functools.partial(far_kernel, scale),
        [narrow, wide, wide],
        "far",
        4e9,
        limit=56,
        blocks={0: only_query, 2: block_at(half_keys, 1, 0)},
    )(
        inputs, member, hidden, far, far_beside, *carry
    )

    feature_count = ordered.shape[1]
    parts = PAIR * CORES
    share = HEAD_DIM // parts
    (partial_sum,) = call(
        outer_kernel, [((parts, share, feature_count), jnp.bfloat16)], "outer", 1e9
    )(attended, group_rows)
    partners = [
        [seat(y, column_of(side, step), at) for side in range(PAIR) for at in range(CORES)]
        for y in range(SIDE)
        for step in range(PAIR)
    ]
    pieces = lax.all_to_all(partial_sum, "seq", 0, 0, axis_index_groups=partners, tiled=True)

    slot = me // (SIDE * CORES) * PAIR + (me // CORES + side) % PAIR
    head_weight = lax.dynamic_slice_in_dim(weight, slot % head_count * HEAD_DIM, HEAD_DIM, axis=0)
    (head_grad,) = call(project_kernel, [narrow], "project", 1e9)(group_rows, head_weight)
    block_count = SLOTS // QUERY_SLOTS

    def backward(blocks, grad, *early):
        shape = ((blocks[-1] + 1) * QUERY_SLOTS, row_count, HEAD_DIM)
        return call(
            functools.partial(grad_kernel, scale, blocks),
            [(shape, jnp.bfloat16)],
            "attend_grad",
            5e9,
            limit=56,
            blocks={0: only_query},
        )(inputs, member, hidden, grad, exact, level, own, beside, far, far_beside, *early)[0]

    early = backward(range(block_count // 2), head_grad)
    pieces, early = lax.optimization_barrier((pieces, early))
    (clip_parts,) = call(
        sum_kernel, [((clip_count, share, feature_count // clip_count), jnp.bfloat16)], "sum", 1e6
    )(pieces)
    clip_parts, head_grad = lax.optimization_barrier((clip_parts, head_grad))
    grad_query = backward(range(block_count // 2, block_count), head_grad, early)
    terms = lax.all_to_all(clip_parts, "dp", 0, 0, tiled=True)
    total = jnp.sum(terms.astype(jnp.float32), axis=0) / float(clip_count)
    total, grad_query = lax.optimization_barrier((total, grad_query))
    total = place_blocks(total, me)
    grad_query = trade(grad_query)
    (grad_query_rows,) = call(
        functools.partial(join_kernel, head_count), [((1, row_count, head_width), jnp.bfloat16)], "join", 1e6
    )(grad_query)
    return (grad_query_rows, total)


def solution(mesh):
    in_specs = (
        P("dp", "seq", None),
        P("dp", "seq", None),
        P("dp", "seq", None),
        P("dp", "seq", None),
        P("dp", None),
        P("dp", None, None),
        P("dp", None),
    )
    out_specs = (P("dp", "seq", None), P("seq", "dp"))
    return jax.shard_map(shards, mesh=mesh, in_specs=in_specs, out_specs=out_specs, check_vma=False)
```

```python
import functools

import jax
import jax.numpy as jnp
from jax import lax
from jax.experimental import pallas as pl
from jax.experimental.pallas import tpu as pltpu
from jax.sharding import PartitionSpec as P

HEAD_DIM = 128
SIDE = 4
CORES = 2
PAIR = 2
SLOTS = SIDE * PAIR
QUERY_SLOTS = 2
KEY_SLOTS = 8
LOG2_E = 1.4426950408889634
HIDDEN = -1e30
LOWEST = -1e20
MIB = 1024 * 1024
NT = (((1,), (1,)), ((), ()))
NN = (((1,), (0,)), ((), ()))
TN = (((0,), (0,)), ((), ()))


def seat(y, x, core):
    return (y % SIDE * SIDE + x % SIDE) * CORES + core % CORES


def column_of(side, step):
    return step if side == 0 else SIDE - 1 - step


def send(value, mirror=False, dcore=0):
    pairs = [
        (seat(y, x, core), seat(y, SIDE - 1 - x if mirror else x, core + dcore))
        for y in range(SIDE)
        for x in range(SIDE)
        for core in range(CORES)
    ]
    return lax.ppermute(value, "seq", pairs)


def trade(slots):
    groups = [
        [seat(y, column_of(side, step), core) for y in range(SIDE) for step in range(PAIR)]
        for side in range(PAIR)
        for core in range(CORES)
    ]
    return lax.all_to_all(slots, "seq", 0, 0, axis_index_groups=groups, tiled=True)


def holders():
    return [
        seat(head // PAIR, column_of(side, head % PAIR), core)
        for head in range(SLOTS - PAIR)
        for side in range(PAIR)
        for core in range(CORES)
    ]


def place_blocks(block, me):
    held = holders()

    def pass_on(routes):
        return lax.ppermute(
            block, "seq", [(held[3 * turn + take], 4 * turn + put) for turn in range(len(held) // 3) for take, put in routes]
        )

    unit = block.shape[0] // 4
    first = pass_on([(0, 0), (1, 1), (2, 3)])
    second = pass_on([(0, 1), (2, 2)])
    third = pass_on([(1, 2)])
    kinds = [
        first[: 3 * unit],
        jnp.concatenate([second[3 * unit :], first[: 2 * unit]]),
        jnp.concatenate([third[2 * unit :], second[:unit]]),
        first[unit:],
    ]
    return lax.select_n(me % 4, *kinds)


def tiles_of(refs):
    return [
        (ref.at[pl.ds(first, KEY_SLOTS), 0], ref.at[pl.ds(first, KEY_SLOTS), 1])
        for ref in refs
        for first in range(0, SLOTS, KEY_SLOTS)
    ]


def rows_of(ref):
    return ref[...].reshape(-1, HEAD_DIM)


def masked_keys(key_ref, hidden_ref, tile):
    rows = KEY_SLOTS * key_ref.shape[1]
    return jnp.concatenate([rows_of(key_ref), hidden_ref[pl.ds(tile * rows, rows), :]], axis=1)


def attend_blocks(scale, input_ref, member_ref, hidden_ref, tiles, start, finish):
    for block in range(SLOTS // QUERY_SLOTS):
        slots = pl.ds(block * QUERY_SLOTS, QUERY_SLOTS)
        query = jnp.concatenate([rows_of(input_ref.at[slots, 0]), rows_of(member_ref.at[slots])], axis=1)
        peak, total = start(slots, query.shape[0])
        for index, (key_ref, value_ref) in enumerate(tiles):
            keys = masked_keys(key_ref, hidden_ref, index)
            values = rows_of(value_ref)
            values = jnp.concatenate([values, jnp.ones_like(values)], axis=1)
            scores = lax.dot_general(query, keys, NT, preferred_element_type=jnp.float32)
            new_peak = jnp.maximum(peak, jnp.max(scores, axis=1, keepdims=True))
            rescale = jnp.exp2((peak - new_peak) * (scale * LOG2_E))
            weights = jnp.exp2((scores - new_peak) * (scale * LOG2_E)).astype(jnp.bfloat16)
            total = total * rescale + lax.dot_general(weights, values, NN, preferred_element_type=jnp.float32)
            peak = new_peak
        finish(block, slots, peak, total)


def split_rows(rows):
    return rows.reshape(QUERY_SLOTS, -1, rows.shape[1])


def near_kernel(scale, input_ref, member_ref, hidden_ref, own_ref, core_ref, peak_ref, total_ref):
    def start(slots, rows):
        return jnp.full((rows, 1), LOWEST, jnp.float32), jnp.zeros((rows, 2 * HEAD_DIM), jnp.float32)

    def finish(block, slots, peak, total):
        peak_ref[slots] = split_rows(peak)
        total_ref[slots] = split_rows(total)

    attend_blocks(scale, input_ref, member_ref, hidden_ref, tiles_of([own_ref, core_ref]), start, finish)


def far_kernel(
    scale, input_ref, member_ref, hidden_ref, own_ref, core_ref, peak_ref, total_ref, attended_ref, exact_ref, level_ref
):
    def start(slots, rows):
        return peak_ref[slots].reshape(rows, 1), total_ref[slots].reshape(rows, 2 * HEAD_DIM)

    def finish(block, slots, peak, total):
        norm = total[:, HEAD_DIM:]
        exact = total[:, :HEAD_DIM] / norm
        attended_ref[slots] = split_rows(exact.astype(jnp.bfloat16))
        exact_ref[slots] = split_rows(exact)
        level_ref[slots] = split_rows(peak * (scale * LOG2_E) + jnp.log2(norm))

    tiles = tiles_of([own_ref, core_ref])
    attend_blocks(scale, input_ref, member_ref, hidden_ref, tiles, start, finish)


def grad_kernel(
    scale, blocks, input_ref, member_ref, hidden_ref, grad_ref, exact_ref, level_ref, own_ref, core_ref, far_ref, far_core_ref, *out_refs
):
    out_ref = out_refs[-1]
    for early_ref in out_refs[:-1]:
        out_ref[pl.ds(0, early_ref.shape[0])] = early_ref[...]
    tiles = tiles_of([own_ref, core_ref, far_ref, far_core_ref])
    for block in blocks:
        slots = pl.ds(block * QUERY_SLOTS, QUERY_SLOTS)
        query = jnp.concatenate([rows_of(input_ref.at[slots, 0]), rows_of(member_ref.at[slots])], axis=1)
        level = rows_of(level_ref.at[slots])
        level = jnp.concatenate([level] * KEY_SLOTS, axis=1)
        grad = rows_of(grad_ref.at[slots])
        centre = jnp.sum(grad.astype(jnp.float32) * rows_of(exact_ref.at[slots]), axis=1, keepdims=True)
        total = jnp.zeros((query.shape[0], HEAD_DIM), jnp.float32)
        for index, (key_ref, value_ref) in enumerate(tiles):
            keys = masked_keys(key_ref, hidden_ref, index)
            scores = lax.dot_general(query, keys, NT, preferred_element_type=jnp.float32)
            probs = jnp.exp2(scores * (scale * LOG2_E) - level)
            grad_probs = lax.dot_general(grad, rows_of(value_ref), NT, preferred_element_type=jnp.float32)
            grad_scores = (probs * (grad_probs - centre)).astype(jnp.bfloat16)
            total = total + lax.dot_general(grad_scores, rows_of(key_ref), NN, preferred_element_type=jnp.float32)
        out_ref[slots] = split_rows((total * scale).astype(jnp.bfloat16))


def project_kernel(rows_ref, weight_ref, out_ref):
    weight = weight_ref[...]
    for slot in range(SLOTS):
        out_ref[slot] = lax.dot_general(rows_ref[slot], weight, NT, preferred_element_type=jnp.float32).astype(
            jnp.bfloat16
        )


def outer_kernel(order_ref, attended_ref, rows_ref, *refs):
    out_refs, held_ref = refs[:-1], refs[-1]
    parts, share, feature_count = held_ref.shape
    attended = attended_ref[...].reshape(-1, HEAD_DIM)
    for first in range(0, feature_count, 4 * HEAD_DIM):
        columns = pl.ds(first, 4 * HEAD_DIM)
        rows = rows_ref[:, :, columns].reshape(attended.shape[0], -1)
        term = lax.dot_general(attended, rows, TN, preferred_element_type=jnp.float32).astype(jnp.bfloat16)
        held_ref[:, :, columns] = term.reshape(parts, share, -1)
    for place, out_ref in enumerate(out_refs):
        out_ref[...] = held_ref[order_ref[place]]


def pack_kernel(head_count, query_ref, key_ref, value_ref, out_ref, sems):
    copies = []
    for slot in range(SLOTS):
        columns = pl.ds(slot % head_count * HEAD_DIM, HEAD_DIM)
        for place, ref in enumerate((query_ref, key_ref, value_ref)):
            copies.append(
                pltpu.make_async_copy(ref.at[0, :, columns], out_ref.at[slot, place], sems.at[slot, place])
            )
    for copy in copies:
        copy.start()
    for copy in copies:
        copy.wait()


def join_kernel(head_count, slots_ref, out_ref):
    for head in range(head_count):
        out_ref[0, :, pl.ds(head * HEAD_DIM, HEAD_DIM)] = slots_ref[head]


def sum_kernel(*refs):
    piece_refs, out_ref = refs[:-1], refs[-1]
    total = piece_refs[0][...].astype(jnp.float32)
    for piece_ref in piece_refs[1:]:
        total = total + piece_ref[...].astype(jnp.float32)
    width = out_ref.shape[2]
    for clip in range(out_ref.shape[0]):
        out_ref[clip] = total[:, clip * width : (clip + 1) * width].astype(jnp.bfloat16)


def block_at(shape, *place):
    return pl.BlockSpec(shape, lambda step: place)


def call(kernel, out_shape, name, flops, scalars=0, **options):
    def run(*operands):
        spaces = [pl.BlockSpec(memory_space=pltpu.SMEM)] * scalars
        spaces = spaces + [pl.BlockSpec()] * (len(operands) - scalars)
        for place, spec in options.get("blocks", {}).items():
            spaces[place] = spec
        return pl.pallas_call(
            kernel,
            out_shape=[jax.ShapeDtypeStruct(shape, dtype) for shape, dtype in out_shape],
            grid=(1,) if "blocks" in options else (),
            in_specs=options.get("in_specs", spaces),
            out_specs=[pl.BlockSpec()] * len(out_shape),
            scratch_shapes=options.get("scratch_shapes", ()),
            compiler_params=pltpu.CompilerParams(vmem_limit_bytes=options.get("limit", 20) * MIB),
            cost_estimate=pl.CostEstimate(flops=int(flops), bytes_accessed=int(1e6), transcendentals=0),
            name=name,
        )(*operands)

    return run


def pack_rows(teacher_rows, counts, me):
    row_count = teacher_rows.shape[0]
    capacity = 2 * row_count // counts.shape[0]
    mine = lax.dynamic_index_in_dim(counts, me, 0, keepdims=False)
    starts = jnp.cumsum(mine) - mine
    slot = jnp.arange(capacity, dtype=jnp.int32)
    source_row = jnp.minimum(starts[:, None] + slot[None, :], row_count - 1)
    return teacher_rows[source_row]


def unpack_rows(arrived, counts, me, row_count):
    peer_count, capacity, feature_count = arrived.shape
    inbound = lax.dynamic_index_in_dim(counts, me, 1, keepdims=False)
    inbound_ends = jnp.cumsum(inbound)
    local_rows = jnp.arange(row_count, dtype=jnp.int32)
    earlier = inbound_ends[None, :] <= local_rows[:, None]
    sender = jnp.sum(earlier.astype(jnp.int32), axis=1)
    offset_in = local_rows - jnp.sum(jnp.where(earlier, inbound[None, :], 0), axis=1)
    return arrived.reshape(peer_count * capacity, feature_count)[sender * capacity + offset_in]


def shards(student_query, key_cache, value_cache, grad_rows, out_weight, return_counts, block_sizes):
    counts = return_counts[0]
    me = lax.axis_index("seq")
    core = me % CORES
    side = me // CORES % SIDE // PAIR
    row_count, head_width = student_query.shape[1:]
    head_count = head_width // HEAD_DIM
    scale = HEAD_DIM ** -0.5
    peer_count = lax.axis_size("seq")
    clip_count = lax.axis_size("dp")
    local_rows = jnp.arange(row_count, dtype=jnp.int32)

    weight = lax.all_gather(out_weight, "dp", axis=0, tiled=True)

    (slots,) = call(
        functools.partial(pack_kernel, head_count),
        [((SLOTS, 3, row_count, HEAD_DIM), jnp.bfloat16)],
        "pack",
        1e6,
        limit=56,
        in_specs=[pl.BlockSpec(memory_space=pl.ANY)] * 3,
        scratch_shapes=[pltpu.SemaphoreType.DMA((SLOTS, 3))],
    )(student_query, key_cache, value_cache)
    inputs = trade(slots)
    inputs, packed = lax.optimization_barrier((inputs, pack_rows(grad_rows[0], counts, me)))
    own = inputs[:, 1:]
    arrived = lax.all_to_all(packed, "seq", 0, 0, tiled=True)
    beside = send(own, dcore=1)

    rank = jnp.arange(SLOTS, dtype=jnp.int32)

    def bases(which_side, which_core):
        column = which_side * (SIDE - 1) + (1 - 2 * which_side) * (rank % PAIR)
        return (((rank // PAIR) * SIDE + column) * CORES + which_core) * row_count

    key_bases = jnp.concatenate(
        [bases(side, core), bases(side, 1 - core), bases(1 - side, core), bases(1 - side, 1 - core)]
    )
    block_ends = jnp.cumsum(block_sizes[0])
    block_starts = block_ends - block_sizes[0]
    pad = HEAD_DIM - block_ends.shape[0]
    ends = jnp.pad(block_ends, (0, pad), constant_values=row_count * peer_count)
    starts = jnp.pad(block_starts, (0, pad), constant_values=row_count * peer_count)
    places = (key_bases[:, None] + local_rows[None, :]).reshape(-1, 1)
    hidden = jnp.where(places < ends[None, :], 0.0, HIDDEN).astype(jnp.bfloat16)
    positions = (bases(side, core)[:, None] + local_rows[None, :])[:, :, None]
    member = ((positions >= starts) & (positions < ends)).astype(jnp.bfloat16)

    column = ((SLOTS, row_count, 1), jnp.float32)
    double = ((SLOTS, row_count, 2 * HEAD_DIM), jnp.float32)
    wide = ((SLOTS, row_count, HEAD_DIM), jnp.float32)
    narrow = ((SLOTS, row_count, HEAD_DIM), jnp.bfloat16)
    only_query = block_at((SLOTS, 1, row_count, HEAD_DIM), 0, 0, 0, 0)
    half_keys = (hidden.shape[0] // 2, HEAD_DIM)
    carry = call(
        functools.partial(near_kernel, scale),
        [column, double],
        "near",
        4e9,
        limit=56,
        blocks={0: only_query, 2: block_at(half_keys, 0, 0)},
    )(
        inputs, member, hidden, own, beside
    )
    ordered = unpack_rows(arrived, counts, me, row_count)
    copies = jnp.broadcast_to(ordered[None], (SLOTS,) + ordered.shape)
    late_own, copies, carry = lax.optimization_barrier((own, copies, carry))
    group_rows = trade(copies)
    far = send(late_own, mirror=True)
    far_beside = send(far, dcore=1)
    attended, exact, level = call(
        functools.partial(far_kernel, scale),
        [narrow, wide, wide],
        "far",
        4e9,
        limit=56,
        blocks={0: only_query, 2: block_at(half_keys, 1, 0)},
    )(
        inputs, member, hidden, far, far_beside, *carry
    )

    feature_count = ordered.shape[1]
    parts = PAIR * CORES
    share = HEAD_DIM // parts
    member_at = side * CORES + core
    order = jnp.stack([member_at ^ step for step in range(parts)])
    pieces = call(
        outer_kernel,
        [((share, feature_count), jnp.bfloat16)] * parts,
        "outer",
        1e9,
        scalars=1,
        scratch_shapes=[pltpu.VMEM((parts, share, feature_count), jnp.bfloat16)],
    )(order, attended, group_rows)
    pieces = [pieces[0]] + [
        send(pieces[step], mirror=step >= CORES, dcore=step % CORES) for step in range(1, parts)
    ]

    slot = me // (SIDE * CORES) * PAIR + (me // CORES + side) % PAIR
    head_weight = lax.dynamic_slice_in_dim(weight, slot % head_count * HEAD_DIM, HEAD_DIM, axis=0)
    (head_grad,) = call(project_kernel, [narrow], "project", 1e9)(group_rows, head_weight)
    block_count = SLOTS // QUERY_SLOTS

    def backward(blocks, grad, *early):
        shape = ((blocks[-1] + 1) * QUERY_SLOTS, row_count, HEAD_DIM)
        return call(
            functools.partial(grad_kernel, scale, blocks),
            [(shape, jnp.bfloat16)],
            "attend_grad",
            5e9,
            limit=56,
            blocks={0: only_query},
        )(inputs, member, hidden, grad, exact, level, own, beside, far, far_beside, *early)[0]

    *pieces, head_grad = lax.optimization_barrier((*pieces, head_grad))
    (clip_parts,) = call(
        sum_kernel, [((clip_count, share, feature_count // clip_count), jnp.bfloat16)], "sum", 1e6
    )(*pieces)
    clip_parts, head_grad = lax.optimization_barrier((clip_parts, head_grad))
    grad_query = backward(range(block_count), head_grad)
    terms = lax.all_to_all(clip_parts, "dp", 0, 0, tiled=True)
    terms, grad_query = lax.optimization_barrier((terms, grad_query))
    total = jnp.sum(terms.astype(jnp.float32), axis=0) / float(clip_count)
    grad_query = trade(grad_query)
    total = place_blocks(total, me)
    (grad_query_rows,) = call(
        functools.partial(join_kernel, head_count), [((1, row_count, head_width), jnp.bfloat16)], "join", 1e6
    )(grad_query)
    return (grad_query_rows, total)


def solution(mesh):
    in_specs = (
        P("dp", "seq", None),
        P("dp", "seq", None),
        P("dp", "seq", None),
        P("dp", "seq", None),
        P("dp", None),
        P("dp", None, None),
        P("dp", None),
    )
    out_specs = (P("dp", "seq", None), P("seq", "dp"))
    return jax.shard_map(shards, mesh=mesh, in_specs=in_specs, out_specs=out_specs, check_vma=False)
```

```python
import functools

import jax
import jax.numpy as jnp
from jax import lax
from jax.experimental import pallas as pl
from jax.experimental.pallas import tpu as pltpu
from jax.sharding import PartitionSpec as P

HEAD_DIM = 128
SIDE = 4
CORES = 2
PAIR = 2
SLOTS = SIDE * PAIR
QUERY_SLOTS = 2
KEY_SLOTS = 8
LOG2_E = 1.4426950408889634
HIDDEN = -1e30
LOWEST = -1e20
MIB = 1024 * 1024
NT = (((1,), (1,)), ((), ()))
NN = (((1,), (0,)), ((), ()))
TN = (((0,), (0,)), ((), ()))


def seat(y, x, core):
    return (y % SIDE * SIDE + x % SIDE) * CORES + core % CORES


def column_of(side, step):
    return step if side == 0 else SIDE - 1 - step


def send(value, mirror=False, dcore=0):
    pairs = [
        (seat(y, x, core), seat(y, SIDE - 1 - x if mirror else x, core + dcore))
        for y in range(SIDE)
        for x in range(SIDE)
        for core in range(CORES)
    ]
    return lax.ppermute(value, "seq", pairs)


def trade(slots):
    groups = [
        [seat(y, column_of(side, step), core) for y in range(SIDE) for step in range(PAIR)]
        for side in range(PAIR)
        for core in range(CORES)
    ]
    return lax.all_to_all(slots, "seq", 0, 0, axis_index_groups=groups, tiled=True)


def holders():
    return [
        seat(head // PAIR, column_of(side, head % PAIR), core)
        for head in range(SLOTS - PAIR)
        for side in range(PAIR)
        for core in range(CORES)
    ]


def place_blocks(block, me):
    held = holders()

    def pass_on(routes):
        return lax.ppermute(
            block, "seq", [(held[3 * turn + take], 4 * turn + put) for turn in range(len(held) // 3) for take, put in routes]
        )

    unit = block.shape[0] // 4
    first = pass_on([(0, 0), (1, 1), (2, 3)])
    second = pass_on([(0, 1), (2, 2)])
    third = pass_on([(1, 2)])
    kinds = [
        first[: 3 * unit],
        jnp.concatenate([second[3 * unit :], first[: 2 * unit]]),
        jnp.concatenate([third[2 * unit :], second[:unit]]),
        first[unit:],
    ]
    return lax.select_n(me % 4, *kinds)


def tiles_of(refs):
    return [
        (ref.at[pl.ds(first, KEY_SLOTS), 0], ref.at[pl.ds(first, KEY_SLOTS), 1])
        for ref in refs
        for first in range(0, SLOTS, KEY_SLOTS)
    ]


def rows_of(ref):
    return ref[...].reshape(-1, HEAD_DIM)


def masked_keys(key_ref, hidden_ref, tile):
    rows = KEY_SLOTS * key_ref.shape[1]
    return jnp.concatenate([rows_of(key_ref), hidden_ref[pl.ds(tile * rows, rows), :]], axis=1)


def attend_blocks(scale, input_ref, member_ref, hidden_ref, tiles, start, finish):
    for block in range(SLOTS // QUERY_SLOTS):
        slots = pl.ds(block * QUERY_SLOTS, QUERY_SLOTS)
        query = jnp.concatenate([rows_of(input_ref.at[slots, 0]), rows_of(member_ref.at[slots])], axis=1)
        peak, total = start(slots, query.shape[0])
        for index, (key_ref, value_ref) in enumerate(tiles):
            keys = masked_keys(key_ref, hidden_ref, index)
            values = rows_of(value_ref)
            values = jnp.concatenate([values, jnp.ones_like(values)], axis=1)
            scores = lax.dot_general(query, keys, NT, preferred_element_type=jnp.float32)
            new_peak = jnp.maximum(peak, jnp.max(scores, axis=1, keepdims=True))
            rescale = jnp.exp2((peak - new_peak) * (scale * LOG2_E))
            weights = jnp.exp2((scores - new_peak) * (scale * LOG2_E)).astype(jnp.bfloat16)
            total = total * rescale + lax.dot_general(weights, values, NN, preferred_element_type=jnp.float32)
            peak = new_peak
        finish(block, slots, peak, total)


def split_rows(rows):
    return rows.reshape(QUERY_SLOTS, -1, rows.shape[1])


def near_kernel(scale, input_ref, member_ref, hidden_ref, own_ref, core_ref, peak_ref, total_ref):
    def start(slots, rows):
        return jnp.full((rows, 1), LOWEST, jnp.float32), jnp.zeros((rows, 2 * HEAD_DIM), jnp.float32)

    def finish(block, slots, peak, total):
        peak_ref[slots] = split_rows(peak)
        total_ref[slots] = split_rows(total)

    attend_blocks(scale, input_ref, member_ref, hidden_ref, tiles_of([own_ref, core_ref]), start, finish)


def far_kernel(
    scale, input_ref, member_ref, hidden_ref, own_ref, core_ref, peak_ref, total_ref, attended_ref, exact_ref, level_ref
):
    def start(slots, rows):
        return peak_ref[slots].reshape(rows, 1), total_ref[slots].reshape(rows, 2 * HEAD_DIM)

    def finish(block, slots, peak, total):
        norm = total[:, HEAD_DIM:]
        exact = total[:, :HEAD_DIM] / norm
        attended_ref[slots] = split_rows(exact.astype(jnp.bfloat16))
        exact_ref[slots] = split_rows(exact)
        level_ref[slots] = split_rows(peak * (scale * LOG2_E) + jnp.log2(norm))

    tiles = tiles_of([own_ref, core_ref])
    attend_blocks(scale, input_ref, member_ref, hidden_ref, tiles, start, finish)


def grad_kernel(
    scale, blocks, input_ref, member_ref, hidden_ref, grad_ref, exact_ref, level_ref, own_ref, core_ref, far_ref, far_core_ref, *out_refs
):
    out_ref = out_refs[-1]
    for early_ref in out_refs[:-1]:
        out_ref[pl.ds(0, early_ref.shape[0])] = early_ref[...]
    tiles = tiles_of([own_ref, core_ref, far_ref, far_core_ref])
    for block in blocks:
        slots = pl.ds(block * QUERY_SLOTS, QUERY_SLOTS)
        query = jnp.concatenate([rows_of(input_ref.at[slots, 0]), rows_of(member_ref.at[slots])], axis=1)
        level = rows_of(level_ref.at[slots])
        level = jnp.concatenate([level] * KEY_SLOTS, axis=1)
        grad = rows_of(grad_ref.at[slots])
        centre = jnp.sum(grad.astype(jnp.float32) * rows_of(exact_ref.at[slots]), axis=1, keepdims=True)
        total = jnp.zeros((query.shape[0], HEAD_DIM), jnp.float32)
        for index, (key_ref, value_ref) in enumerate(tiles):
            keys = masked_keys(key_ref, hidden_ref, index)
            scores = lax.dot_general(query, keys, NT, preferred_element_type=jnp.float32)
            probs = jnp.exp2(scores * (scale * LOG2_E) - level)
            grad_probs = lax.dot_general(grad, rows_of(value_ref), NT, preferred_element_type=jnp.float32)
            grad_scores = (probs * (grad_probs - centre)).astype(jnp.bfloat16)
            total = total + lax.dot_general(grad_scores, rows_of(key_ref), NN, preferred_element_type=jnp.float32)
        out_ref[slots] = split_rows((total * scale).astype(jnp.bfloat16))


def project_kernel(rows_ref, weight_ref, out_ref):
    weight = weight_ref[...]
    for slot in range(SLOTS):
        out_ref[slot] = lax.dot_general(rows_ref[slot], weight, NT, preferred_element_type=jnp.float32).astype(
            jnp.bfloat16
        )


def outer_kernel(order_ref, attended_ref, rows_ref, *refs):
    out_refs, held_ref = refs[:-1], refs[-1]
    parts, share, feature_count = held_ref.shape
    attended = attended_ref[...].reshape(-1, HEAD_DIM)
    for first in range(0, feature_count, 4 * HEAD_DIM):
        columns = pl.ds(first, 4 * HEAD_DIM)
        rows = rows_ref[:, :, columns].reshape(attended.shape[0], -1)
        term = lax.dot_general(attended, rows, TN, preferred_element_type=jnp.float32).astype(jnp.bfloat16)
        held_ref[:, :, columns] = term.reshape(parts, share, -1)
    for place, out_ref in enumerate(out_refs):
        out_ref[...] = held_ref[order_ref[place]]


def pack_kernel(head_count, query_ref, key_ref, value_ref, out_ref, sems):
    copies = []
    for slot in range(SLOTS):
        columns = pl.ds(slot % head_count * HEAD_DIM, HEAD_DIM)
        for place, ref in enumerate((query_ref, key_ref, value_ref)):
            copies.append(
                pltpu.make_async_copy(ref.at[0, :, columns], out_ref.at[slot, place], sems.at[slot, place])
            )
    for copy in copies:
        copy.start()
    for copy in copies:
        copy.wait()


def copy_kernel(rows_ref, out_ref):
    for slot in range(SLOTS):
        out_ref[slot] = rows_ref[...]


def join_kernel(head_count, slots_ref, out_ref):
    for head in range(head_count):
        out_ref[0, :, pl.ds(head * HEAD_DIM, HEAD_DIM)] = slots_ref[head]


def sum_kernel(*refs):
    piece_refs, out_ref = refs[:-1], refs[-1]
    total = piece_refs[0][...].astype(jnp.float32)
    for piece_ref in piece_refs[1:]:
        total = total + piece_ref[...].astype(jnp.float32)
    width = out_ref.shape[2]
    for clip in range(out_ref.shape[0]):
        out_ref[clip] = total[:, clip * width : (clip + 1) * width].astype(jnp.bfloat16)


def block_at(shape, *place):
    return pl.BlockSpec(shape, lambda step: place)


def call(kernel, out_shape, name, flops, scalars=0, **options):
    def run(*operands):
        spaces = [pl.BlockSpec(memory_space=pltpu.SMEM)] * scalars
        spaces = spaces + [pl.BlockSpec()] * (len(operands) - scalars)
        for place, spec in options.get("blocks", {}).items():
            spaces[place] = spec
        return pl.pallas_call(
            kernel,
            out_shape=[jax.ShapeDtypeStruct(shape, dtype) for shape, dtype in out_shape],
            grid=(1,) if "blocks" in options else (),
            in_specs=options.get("in_specs", spaces),
            out_specs=[pl.BlockSpec()] * len(out_shape),
            scratch_shapes=options.get("scratch_shapes", ()),
            compiler_params=pltpu.CompilerParams(vmem_limit_bytes=options.get("limit", 20) * MIB),
            cost_estimate=pl.CostEstimate(flops=int(flops), bytes_accessed=int(1e6), transcendentals=0),
            name=name,
        )(*operands)

    return run


def pack_rows(teacher_rows, counts, me):
    row_count = teacher_rows.shape[0]
    capacity = 2 * row_count // counts.shape[0]
    mine = lax.dynamic_index_in_dim(counts, me, 0, keepdims=False)
    starts = jnp.cumsum(mine) - mine
    slot = jnp.arange(capacity, dtype=jnp.int32)
    source_row = jnp.minimum(starts[:, None] + slot[None, :], row_count - 1)
    return teacher_rows[source_row]


def unpack_rows(arrived, counts, me, row_count):
    peer_count, capacity, feature_count = arrived.shape
    inbound = lax.dynamic_index_in_dim(counts, me, 1, keepdims=False)
    inbound_ends = jnp.cumsum(inbound)
    local_rows = jnp.arange(row_count, dtype=jnp.int32)
    earlier = inbound_ends[None, :] <= local_rows[:, None]
    sender = jnp.sum(earlier.astype(jnp.int32), axis=1)
    offset_in = local_rows - jnp.sum(jnp.where(earlier, inbound[None, :], 0), axis=1)
    return arrived.reshape(peer_count * capacity, feature_count)[sender * capacity + offset_in]


def shards(student_query, key_cache, value_cache, grad_rows, out_weight, return_counts, block_sizes):
    counts = return_counts[0]
    me = lax.axis_index("seq")
    core = me % CORES
    side = me // CORES % SIDE // PAIR
    row_count, head_width = student_query.shape[1:]
    head_count = head_width // HEAD_DIM
    scale = HEAD_DIM ** -0.5
    peer_count = lax.axis_size("seq")
    clip_count = lax.axis_size("dp")
    local_rows = jnp.arange(row_count, dtype=jnp.int32)

    weight = lax.all_gather(out_weight, "dp", axis=0, tiled=True)

    (slots,) = call(
        functools.partial(pack_kernel, head_count),
        [((SLOTS, 3, row_count, HEAD_DIM), jnp.bfloat16)],
        "pack",
        1e6,
        limit=56,
        in_specs=[pl.BlockSpec(memory_space=pl.ANY)] * 3,
        scratch_shapes=[pltpu.SemaphoreType.DMA((SLOTS, 3))],
    )(student_query, key_cache, value_cache)
    arrived = lax.all_to_all(pack_rows(grad_rows[0], counts, me), "seq", 0, 0, tiled=True)
    slots, arrived = lax.optimization_barrier((slots, arrived))
    inputs = trade(slots)
    own = inputs[:, 1:]
    beside = send(own, dcore=1)

    rank = jnp.arange(SLOTS, dtype=jnp.int32)

    def bases(which_side, which_core):
        column = which_side * (SIDE - 1) + (1 - 2 * which_side) * (rank % PAIR)
        return (((rank // PAIR) * SIDE + column) * CORES + which_core) * row_count

    key_bases = jnp.concatenate(
        [bases(side, core), bases(side, 1 - core), bases(1 - side, core), bases(1 - side, 1 - core)]
    )
    block_ends = jnp.cumsum(block_sizes[0])
    block_starts = block_ends - block_sizes[0]
    pad = HEAD_DIM - block_ends.shape[0]
    ends = jnp.pad(block_ends, (0, pad), constant_values=row_count * peer_count)
    starts = jnp.pad(block_starts, (0, pad), constant_values=row_count * peer_count)
    places = (key_bases[:, None] + local_rows[None, :]).reshape(-1, 1)
    hidden = jnp.where(places < ends[None, :], 0.0, HIDDEN).astype(jnp.bfloat16)
    positions = (bases(side, core)[:, None] + local_rows[None, :])[:, :, None]
    member = ((positions >= starts) & (positions < ends)).astype(jnp.bfloat16)

    column = ((SLOTS, row_count, 1), jnp.float32)
    double = ((SLOTS, row_count, 2 * HEAD_DIM), jnp.float32)
    wide = ((SLOTS, row_count, HEAD_DIM), jnp.float32)
    narrow = ((SLOTS, row_count, HEAD_DIM), jnp.bfloat16)
    only_query = block_at((SLOTS, 1, row_count, HEAD_DIM), 0, 0, 0, 0)
    half_keys = (hidden.shape[0] // 2, HEAD_DIM)
    carry = call(
        functools.partial(near_kernel, scale),
        [column, double],
        "near",
        4e9,
        limit=56,
        blocks={0: only_query, 2: block_at(half_keys, 0, 0)},
    )(
        inputs, member, hidden, own, beside
    )
    ordered = unpack_rows(arrived, counts, me, row_count)
    (copies,) = call(copy_kernel, [((SLOTS,) + ordered.shape, jnp.bfloat16)], "copies", 8e9)(ordered)
    late_own, copies = lax.optimization_barrier((own, copies))
    group_rows = trade(copies)
    far = send(late_own, mirror=True)
    far, carry = lax.optimization_barrier((far, carry))
    far_beside = send(far, dcore=1)
    attended, exact, level = call(
        functools.partial(far_kernel, scale),
        [narrow, wide, wide],
        "far",
        4e9,
        limit=56,
        blocks={0: only_query, 2: block_at(half_keys, 1, 0)},
    )(
        inputs, member, hidden, far, far_beside, *carry
    )

    feature_count = ordered.shape[1]
    parts = PAIR * CORES
    share = HEAD_DIM // parts
    member_at = side * CORES + core
    order = jnp.stack([member_at ^ step for step in range(parts)])
    pieces = call(
        outer_kernel,
        [((share, feature_count), jnp.bfloat16)] * parts,
        "outer",
        1e9,
        scalars=1,
        scratch_shapes=[pltpu.VMEM((parts, share, feature_count), jnp.bfloat16)],
    )(order, attended, group_rows)
    pieces = [pieces[0]] + [
        send(pieces[step], mirror=step >= CORES, dcore=step % CORES) for step in range(1, parts)
    ]

    slot = me // (SIDE * CORES) * PAIR + (me // CORES + side) % PAIR
    head_weight = lax.dynamic_slice_in_dim(weight, slot % head_count * HEAD_DIM, HEAD_DIM, axis=0)
    (head_grad,) = call(project_kernel, [narrow], "project", 1e9)(group_rows, head_weight)
    block_count = SLOTS // QUERY_SLOTS

    def backward(blocks, grad, *early):
        shape = ((blocks[-1] + 1) * QUERY_SLOTS, row_count, HEAD_DIM)
        return call(
            functools.partial(grad_kernel, scale, blocks),
            [(shape, jnp.bfloat16)],
            "attend_grad",
            5e9,
            limit=56,
            blocks={0: only_query},
        )(inputs, member, hidden, grad, exact, level, own, beside, far, far_beside, *early)[0]

    *pieces, head_grad = lax.optimization_barrier((*pieces, head_grad))
    (clip_parts,) = call(
        sum_kernel, [((clip_count, share, feature_count // clip_count), jnp.bfloat16)], "sum", 1e6
    )(*pieces)
    clip_parts, head_grad = lax.optimization_barrier((clip_parts, head_grad))
    grad_query = backward(range(block_count), head_grad)
    terms = lax.all_to_all(clip_parts, "dp", 0, 0, tiled=True)
    terms, grad_query = lax.optimization_barrier((terms, grad_query))
    total = jnp.sum(terms.astype(jnp.float32), axis=0) / float(clip_count)
    grad_query = trade(grad_query)
    total = place_blocks(total, me)
    (grad_query_rows,) = call(
        functools.partial(join_kernel, head_count), [((1, row_count, head_width), jnp.bfloat16)], "join", 1e6
    )(grad_query)
    return (grad_query_rows, total)


def solution(mesh):
    in_specs = (
        P("dp", "seq", None),
        P("dp", "seq", None),
        P("dp", "seq", None),
        P("dp", "seq", None),
        P("dp", None),
        P("dp", None, None),
        P("dp", None),
    )
    out_specs = (P("dp", "seq", None), P("seq", "dp"))
    return jax.shard_map(shards, mesh=mesh, in_specs=in_specs, out_specs=out_specs, check_vma=False)
```

```python
import functools

import jax
import jax.numpy as jnp
from jax import lax
from jax.experimental import pallas as pl
from jax.experimental.pallas import tpu as pltpu
from jax.sharding import PartitionSpec as P

HEAD_DIM = 128
SIDE = 4
CORES = 2
PAIR = 2
SLOTS = SIDE * PAIR
QUERY_SLOTS = 2
KEY_SLOTS = 8
LOG2_E = 1.4426950408889634
HIDDEN = -1e30
LOWEST = -1e20
MIB = 1024 * 1024
NT = (((1,), (1,)), ((), ()))
NN = (((1,), (0,)), ((), ()))
TN = (((0,), (0,)), ((), ()))


def seat(y, x, core):
    return (y % SIDE * SIDE + x % SIDE) * CORES + core % CORES


def column_of(side, step):
    return step if side == 0 else SIDE - 1 - step


def send(value, mirror=False, dcore=0):
    pairs = [
        (seat(y, x, core), seat(y, SIDE - 1 - x if mirror else x, core + dcore))
        for y in range(SIDE)
        for x in range(SIDE)
        for core in range(CORES)
    ]
    return lax.ppermute(value, "seq", pairs)


def trade(slots):
    groups = [
        [seat(y, column_of(side, step), core) for y in range(SIDE) for step in range(PAIR)]
        for side in range(PAIR)
        for core in range(CORES)
    ]
    return lax.all_to_all(slots, "seq", 0, 0, axis_index_groups=groups, tiled=True)


def holders():
    return [
        seat(head // PAIR, column_of(side, head % PAIR), core)
        for head in range(SLOTS - PAIR)
        for side in range(PAIR)
        for core in range(CORES)
    ]


def place_blocks(block, me):
    held = holders()

    def pass_on(routes):
        return lax.ppermute(
            block, "seq", [(held[3 * turn + take], 4 * turn + put) for turn in range(len(held) // 3) for take, put in routes]
        )

    unit = block.shape[0] // 4
    first = pass_on([(0, 0), (1, 1), (2, 3)])
    second = pass_on([(0, 1), (2, 2)])
    third = pass_on([(1, 2)])
    kinds = [
        first[: 3 * unit],
        jnp.concatenate([second[3 * unit :], first[: 2 * unit]]),
        jnp.concatenate([third[2 * unit :], second[:unit]]),
        first[unit:],
    ]
    return lax.select_n(me % 4, *kinds)


def tiles_of(refs):
    return [
        (ref.at[pl.ds(first, KEY_SLOTS), 0], ref.at[pl.ds(first, KEY_SLOTS), 1])
        for ref in refs
        for first in range(0, SLOTS, KEY_SLOTS)
    ]


def rows_of(ref):
    return ref[...].reshape(-1, HEAD_DIM)


def masked_keys(key_ref, hidden_ref, tile):
    rows = KEY_SLOTS * key_ref.shape[1]
    return jnp.concatenate([rows_of(key_ref), hidden_ref[pl.ds(tile * rows, rows), :]], axis=1)


def attend_blocks(scale, input_ref, member_ref, hidden_ref, tiles, start, finish):
    for block in range(SLOTS // QUERY_SLOTS):
        slots = pl.ds(block * QUERY_SLOTS, QUERY_SLOTS)
        query = jnp.concatenate([rows_of(input_ref.at[slots, 0]), rows_of(member_ref.at[slots])], axis=1)
        peak, total = start(slots, query.shape[0])
        for index, (key_ref, value_ref) in enumerate(tiles):
            keys = masked_keys(key_ref, hidden_ref, index)
            values = rows_of(value_ref)
            values = jnp.concatenate([values, jnp.ones_like(values)], axis=1)
            scores = lax.dot_general(query, keys, NT, preferred_element_type=jnp.float32)
            new_peak = jnp.maximum(peak, jnp.max(scores, axis=1, keepdims=True))
            rescale = jnp.exp2((peak - new_peak) * (scale * LOG2_E))
            weights = jnp.exp2((scores - new_peak) * (scale * LOG2_E)).astype(jnp.bfloat16)
            total = total * rescale + lax.dot_general(weights, values, NN, preferred_element_type=jnp.float32)
            peak = new_peak
        finish(block, slots, peak, total)


def split_rows(rows):
    return rows.reshape(QUERY_SLOTS, -1, rows.shape[1])


def near_kernel(scale, input_ref, member_ref, hidden_ref, own_ref, core_ref, peak_ref, total_ref):
    def start(slots, rows):
        return jnp.full((rows, 1), LOWEST, jnp.float32), jnp.zeros((rows, 2 * HEAD_DIM), jnp.float32)

    def finish(block, slots, peak, total):
        peak_ref[slots] = split_rows(peak)
        total_ref[slots] = split_rows(total)

    attend_blocks(scale, input_ref, member_ref, hidden_ref, tiles_of([own_ref, core_ref]), start, finish)


def far_kernel(
    scale, input_ref, member_ref, hidden_ref, own_ref, core_ref, peak_ref, total_ref, attended_ref, exact_ref, level_ref
):
    def start(slots, rows):
        return peak_ref[slots].reshape(rows, 1), total_ref[slots].reshape(rows, 2 * HEAD_DIM)

    def finish(block, slots, peak, total):
        norm = total[:, HEAD_DIM:]
        exact = total[:, :HEAD_DIM] / norm
        attended_ref[slots] = split_rows(exact.astype(jnp.bfloat16))
        exact_ref[slots] = split_rows(exact)
        level_ref[slots] = split_rows(peak * (scale * LOG2_E) + jnp.log2(norm))

    tiles = tiles_of([own_ref, core_ref])
    attend_blocks(scale, input_ref, member_ref, hidden_ref, tiles, start, finish)


def grad_kernel(
    scale, blocks, input_ref, member_ref, hidden_ref, grad_ref, exact_ref, level_ref, own_ref, core_ref, far_ref, far_core_ref, *out_refs
):
    out_ref = out_refs[-1]
    for early_ref in out_refs[:-1]:
        out_ref[pl.ds(0, early_ref.shape[0])] = early_ref[...]
    tiles = tiles_of([own_ref, core_ref, far_ref, far_core_ref])
    for block in blocks:
        slots = pl.ds(block * QUERY_SLOTS, QUERY_SLOTS)
        query = jnp.concatenate([rows_of(input_ref.at[slots, 0]), rows_of(member_ref.at[slots])], axis=1)
        level = rows_of(level_ref.at[slots])
        level = jnp.concatenate([level] * KEY_SLOTS, axis=1)
        grad = rows_of(grad_ref.at[slots])
        centre = jnp.sum(grad.astype(jnp.float32) * rows_of(exact_ref.at[slots]), axis=1, keepdims=True)
        total = jnp.zeros((query.shape[0], HEAD_DIM), jnp.float32)
        for index, (key_ref, value_ref) in enumerate(tiles):
            keys = masked_keys(key_ref, hidden_ref, index)
            scores = lax.dot_general(query, keys, NT, preferred_element_type=jnp.float32)
            probs = jnp.exp2(scores * (scale * LOG2_E) - level)
            grad_probs = lax.dot_general(grad, rows_of(value_ref), NT, preferred_element_type=jnp.float32)
            grad_scores = (probs * (grad_probs - centre)).astype(jnp.bfloat16)
            total = total + lax.dot_general(grad_scores, rows_of(key_ref), NN, preferred_element_type=jnp.float32)
        out_ref[slots] = split_rows((total * scale).astype(jnp.bfloat16))


def project_kernel(rows_ref, weight_ref, out_ref):
    weight = weight_ref[...]
    for slot in range(SLOTS):
        out_ref[slot] = lax.dot_general(rows_ref[slot], weight, NT, preferred_element_type=jnp.float32).astype(
            jnp.bfloat16
        )


def outer_kernel(order_ref, attended_ref, rows_ref, *refs):
    out_refs, held_ref = refs[:-1], refs[-1]
    parts, share, feature_count = held_ref.shape
    attended = attended_ref[...].reshape(-1, HEAD_DIM)
    for first in range(0, feature_count, 4 * HEAD_DIM):
        columns = pl.ds(first, 4 * HEAD_DIM)
        rows = rows_ref[:, :, columns].reshape(attended.shape[0], -1)
        term = lax.dot_general(attended, rows, TN, preferred_element_type=jnp.float32).astype(jnp.bfloat16)
        held_ref[:, :, columns] = term.reshape(parts, share, -1)
    for place, out_ref in enumerate(out_refs):
        out_ref[...] = held_ref[order_ref[place]]


def pack_kernel(head_count, query_ref, key_ref, value_ref, out_ref, sems):
    copies = []
    for slot in range(SLOTS):
        columns = pl.ds(slot % head_count * HEAD_DIM, HEAD_DIM)
        for place, ref in enumerate((query_ref, key_ref, value_ref)):
            copies.append(
                pltpu.make_async_copy(ref.at[0, :, columns], out_ref.at[slot, place], sems.at[slot, place])
            )
    for copy in copies:
        copy.start()
    for copy in copies:
        copy.wait()


def join_kernel(head_count, slots_ref, out_ref):
    for head in range(head_count):
        out_ref[0, :, pl.ds(head * HEAD_DIM, HEAD_DIM)] = slots_ref[head]


def sum_kernel(*refs):
    piece_refs, out_ref = refs[:-1], refs[-1]
    total = piece_refs[0][...].astype(jnp.float32)
    for piece_ref in piece_refs[1:]:
        total = total + piece_ref[...].astype(jnp.float32)
    width = out_ref.shape[2]
    for clip in range(out_ref.shape[0]):
        out_ref[clip] = total[:, clip * width : (clip + 1) * width].astype(jnp.bfloat16)


def block_at(shape, *place):
    return pl.BlockSpec(shape, lambda step: place)


def call(kernel, out_shape, name, flops, scalars=0, **options):
    def run(*operands):
        spaces = [pl.BlockSpec(memory_space=pltpu.SMEM)] * scalars
        spaces = spaces + [pl.BlockSpec()] * (len(operands) - scalars)
        for place, spec in options.get("blocks", {}).items():
            spaces[place] = spec
        return pl.pallas_call(
            kernel,
            out_shape=[jax.ShapeDtypeStruct(shape, dtype) for shape, dtype in out_shape],
            grid=(1,) if "blocks" in options else (),
            in_specs=options.get("in_specs", spaces),
            out_specs=[pl.BlockSpec()] * len(out_shape),
            scratch_shapes=options.get("scratch_shapes", ()),
            compiler_params=pltpu.CompilerParams(vmem_limit_bytes=options.get("limit", 20) * MIB),
            cost_estimate=pl.CostEstimate(flops=int(flops), bytes_accessed=int(1e6), transcendentals=0),
            name=name,
        )(*operands)

    return run


def pack_rows(teacher_rows, counts, me):
    row_count = teacher_rows.shape[0]
    capacity = 2 * row_count // counts.shape[0]
    mine = lax.dynamic_index_in_dim(counts, me, 0, keepdims=False)
    starts = jnp.cumsum(mine) - mine
    slot = jnp.arange(capacity, dtype=jnp.int32)
    source_row = jnp.minimum(starts[:, None] + slot[None, :], row_count - 1)
    return teacher_rows[source_row]


def unpack_rows(arrived, counts, me, row_count):
    peer_count, capacity, feature_count = arrived.shape
    inbound = lax.dynamic_index_in_dim(counts, me, 1, keepdims=False)
    inbound_ends = jnp.cumsum(inbound)
    local_rows = jnp.arange(row_count, dtype=jnp.int32)
    earlier = inbound_ends[None, :] <= local_rows[:, None]
    sender = jnp.sum(earlier.astype(jnp.int32), axis=1)
    offset_in = local_rows - jnp.sum(jnp.where(earlier, inbound[None, :], 0), axis=1)
    return arrived.reshape(peer_count * capacity, feature_count)[sender * capacity + offset_in]


def shards(student_query, key_cache, value_cache, grad_rows, out_weight, return_counts, block_sizes):
    counts = return_counts[0]
    me = lax.axis_index("seq")
    core = me % CORES
    side = me // CORES % SIDE // PAIR
    row_count, head_width = student_query.shape[1:]
    head_count = head_width // HEAD_DIM
    scale = HEAD_DIM ** -0.5
    peer_count = lax.axis_size("seq")
    clip_count = lax.axis_size("dp")
    local_rows = jnp.arange(row_count, dtype=jnp.int32)

    weight = lax.all_gather(out_weight, "dp", axis=0, tiled=True)

    (slots,) = call(
        functools.partial(pack_kernel, head_count),
        [((SLOTS, 3, row_count, HEAD_DIM), jnp.bfloat16)],
        "pack",
        1e6,
        limit=56,
        in_specs=[pl.BlockSpec(memory_space=pl.ANY)] * 3,
        scratch_shapes=[pltpu.SemaphoreType.DMA((SLOTS, 3))],
    )(student_query, key_cache, value_cache)
    inputs = trade(slots)
    inputs, packed = lax.optimization_barrier((inputs, pack_rows(grad_rows[0], counts, me)))
    own = inputs[:, 1:]
    arrived = lax.all_to_all(packed, "seq", 0, 0, tiled=True)
    beside = send(own, dcore=1)

    rank = jnp.arange(SLOTS, dtype=jnp.int32)

    def bases(which_side, which_core):
        column = which_side * (SIDE - 1) + (1 - 2 * which_side) * (rank % PAIR)
        return (((rank // PAIR) * SIDE + column) * CORES + which_core) * row_count

    key_bases = jnp.concatenate(
        [bases(side, core), bases(side, 1 - core), bases(1 - side, core), bases(1 - side, 1 - core)]
    )
    block_ends = jnp.cumsum(block_sizes[0])
    block_starts = block_ends - block_sizes[0]
    pad = HEAD_DIM - block_ends.shape[0]
    ends = jnp.pad(block_ends, (0, pad), constant_values=row_count * peer_count)
    starts = jnp.pad(block_starts, (0, pad), constant_values=row_count * peer_count)
    places = (key_bases[:, None] + local_rows[None, :]).reshape(-1, 1)
    hidden = jnp.where(places < ends[None, :], 0.0, HIDDEN).astype(jnp.bfloat16)
    positions = (bases(side, core)[:, None] + local_rows[None, :])[:, :, None]
    member = ((positions >= starts) & (positions < ends)).astype(jnp.bfloat16)

    column = ((SLOTS, row_count, 1), jnp.float32)
    double = ((SLOTS, row_count, 2 * HEAD_DIM), jnp.float32)
    wide = ((SLOTS, row_count, HEAD_DIM), jnp.float32)
    narrow = ((SLOTS, row_count, HEAD_DIM), jnp.bfloat16)
    only_query = block_at((SLOTS, 1, row_count, HEAD_DIM), 0, 0, 0, 0)
    half_keys = (hidden.shape[0] // 2, HEAD_DIM)
    carry = call(
        functools.partial(near_kernel, scale),
        [column, double],
        "near",
        4e9,
        limit=56,
        blocks={0: only_query, 2: block_at(half_keys, 0, 0)},
    )(
        inputs, member, hidden, own, beside
    )
    ordered = unpack_rows(arrived, counts, me, row_count)
    copies = jnp.broadcast_to(ordered[None], (SLOTS,) + ordered.shape)
    late_own, copies, carry = lax.optimization_barrier((own, copies, carry))
    group_rows = trade(copies)
    far = send(late_own, mirror=True)
    far_beside = send(far, dcore=1)
    attended, exact, level = call(
        functools.partial(far_kernel, scale),
        [narrow, wide, wide],
        "far",
        4e9,
        limit=56,
        blocks={0: only_query, 2: block_at(half_keys, 1, 0)},
    )(
        inputs, member, hidden, far, far_beside, *carry
    )

    feature_count = ordered.shape[1]
    parts = PAIR * CORES
    share = HEAD_DIM // parts
    member_at = side * CORES + core
    order = jnp.stack([member_at ^ step for step in range(parts)])
    pieces = call(
        outer_kernel,
        [((share, feature_count), jnp.bfloat16)] * parts,
        "outer",
        1e9,
        scalars=1,
        scratch_shapes=[pltpu.VMEM((parts, share, feature_count), jnp.bfloat16)],
    )(order, attended, group_rows)
    pieces = [pieces[0]] + [
        send(pieces[step], mirror=step >= CORES, dcore=step % CORES) for step in range(1, parts)
    ]

    slot = me // (SIDE * CORES) * PAIR + (me // CORES + side) % PAIR
    head_weight = lax.dynamic_slice_in_dim(weight, slot % head_count * HEAD_DIM, HEAD_DIM, axis=0)
    (head_grad,) = call(project_kernel, [narrow], "project", 1e9)(group_rows, head_weight)
    block_count = SLOTS // QUERY_SLOTS

    def backward(blocks, grad, *early):
        shape = ((blocks[-1] + 1) * QUERY_SLOTS, row_count, HEAD_DIM)
        return call(
            functools.partial(grad_kernel, scale, blocks),
            [(shape, jnp.bfloat16)],
            "attend_grad",
            5e9,
            limit=56,
            blocks={0: only_query},
        )(inputs, member, hidden, grad, exact, level, own, beside, far, far_beside, *early)[0]

    *pieces, head_grad = lax.optimization_barrier((*pieces, head_grad))
    (clip_parts,) = call(
        sum_kernel, [((clip_count, share, feature_count // clip_count), jnp.bfloat16)], "sum", 1e6
    )(*pieces)
    clip_parts, head_grad = lax.optimization_barrier((clip_parts, head_grad))
    grad_query = backward(range(block_count), head_grad)
    terms = lax.all_to_all(clip_parts, "dp", 0, 0, tiled=True)
    terms, grad_query = lax.optimization_barrier((terms, grad_query))
    total = jnp.sum(terms.astype(jnp.float32), axis=0) / float(clip_count)
    grad_query = trade(grad_query)
    total, grad_query = lax.optimization_barrier((total, grad_query))
    total = place_blocks(total, me)
    (grad_query_rows,) = call(
        functools.partial(join_kernel, head_count), [((1, row_count, head_width), jnp.bfloat16)], "join", 1e6
    )(grad_query)
    return (grad_query_rows, total)


def solution(mesh):
    in_specs = (
        P("dp", "seq", None),
        P("dp", "seq", None),
        P("dp", "seq", None),
        P("dp", "seq", None),
        P("dp", None),
        P("dp", None, None),
        P("dp", None),
    )
    out_specs = (P("dp", "seq", None), P("seq", "dp"))
    return jax.shard_map(shards, mesh=mesh, in_specs=in_specs, out_specs=out_specs, check_vma=False)
```
